512 devices in a mesh: layer: 4 (over y), prow: 16 (over z), pcol: 8 (over x, core).
Axes of the slice: x: 4, y: 4, z: 16, core: 2. Of those that a mesh axis runs over, the one named last changes fastest.
Arguments:
- own_blocks: bfloat16 [4, 21, 16, 128, 2, 8, 128], P('layer', None, 'prow', None, None, 'pcol'), may hold values from -0.046875 to 0.046875
- own_pattern: int32 [4, 21, 16, 2, 8], P('layer', None, 'prow', None, 'pcol'), may hold values 0 or 1
- own_inverse: bfloat16 [4, 3, 16, 128, 2, 8, 128], P('layer', None, 'prow', None, None, 'pcol'), as said below
- pair_blocks: bfloat16 [4, 12, 16, 128, 2, 8, 128], P('layer', None, 'prow', None, None, 'pcol'), as said below
- pair_inverse: bfloat16 [4, 3, 16, 128, 2, 8, 128], P('layer', None, 'prow', None, None, 'pcol'), as said below
- root_blocks: bfloat16 [3, 16, 128, 2, 8, 128], P(None, 'prow', None, None, 'pcol'), may hold values from -0.046875 to 0.046875
- root_inverse: bfloat16 [3, 16, 128, 2, 8, 128], P(None, 'prow', None, None, 'pcol'), as said below
- own_rhs: bfloat16 [4, 3, 16, 128, 256], P('layer', None, 'prow'), may hold values from -6 to 6
- shared_rhs: bfloat16 [4, 6, 16, 128, 256], P('layer', None, 'prow'), may hold values from -3 to 3
Outputs:
- own_solution: bfloat16 [4, 3, 2, 8, 128, 256], P('layer', None, None, 'pcol')
- pair_solution: bfloat16 [4, 3, 2, 8, 128, 256], P('layer', None, None, 'pcol')
- root_solution: bfloat16 [4, 3, 2, 8, 128, 256], P('layer', None, None, 'pcol')
The draws below stay inside these ranges and needn't reach their ends.
Inputs may be any that keep to these rules, and one draw needn't show every extreme that they name: `pair_blocks`: layers 2m and 2m+1 hold equal copies of their parent's blocks. `pair_inverse`: each panel's inverse is lower triangular; layers 2m and 2m+1 hold equal copies. `own_inverse`: each panel's inverse is lower triangular. `root_inverse`: each panel's inverse is lower triangular.
All inputs are finite; a program needn't handle non-finite values. No bound on the sum of `own_pattern` on one device may be relied on, other than what follows from the above.
Results may differ from the reference program's by a relative error of at most 0.038.
Values may be sent and summed in bfloat16 or wider, within the bound.
No kernel may reach another device: no remote copies, remote signals or barrier semaphores. Data moves between devices by JAX's collectives and lax.ppermute only.
A program may use at most 64 MiB of HBM per device.

```python
import jax
import jax.numpy as jnp
from jax import lax

NB = 128
NRHS = 256
SP = 3
CY = 2
PW = 2048
NOWN = 21
NPAIR = 12
NROOT = 3
N_LAYER = 4
N_PROW = 16
N_PCOL = 8


def tiled_inverse(key, leading):
    shape = leading + (N_PROW, NB, CY, N_PCOL, NB)
    column_index = jnp.arange(N_PROW).reshape(N_PROW, 1, 1, 1, 1) * NB + jnp.arange(NB).reshape(1, NB, 1, 1, 1)
    tile_index = jnp.arange(CY).reshape(1, 1, CY, 1, 1) * N_PCOL + jnp.arange(N_PCOL).reshape(1, 1, 1, N_PCOL, 1)
    row_index = tile_index * NB + jnp.arange(NB).reshape(1, 1, 1, 1, NB)
    lower_part = jax.random.truncated_normal(jax.random.fold_in(key, 11), -4.0, 4.0, shape, jnp.float32) * (0.8 / PW ** 0.5)
    diagonal = jax.random.uniform(jax.random.fold_in(key, 12), shape, jnp.float32, 0.7, 1.3)
    return jnp.where(row_index > column_index, lower_part, jnp.where(row_index == column_index, diagonal, 0.0))


def draw_own_inverse(key, part):
    return tiled_inverse(key, (N_LAYER, SP)).astype(jnp.bfloat16)


def draw_pair_inverse(key, part):
    copies = tiled_inverse(key, (N_LAYER // 2, SP))
    return jnp.repeat(copies, 2, axis=0).astype(jnp.bfloat16)


def draw_root_inverse(key, part):
    return tiled_inverse(key, (SP,)).astype(jnp.bfloat16)


def draw_pair_blocks(key, part):
    shape = (N_LAYER // 2, NPAIR, N_PROW, NB, CY, N_PCOL, NB)
    copies = jax.random.truncated_normal(key, -4.0, 4.0, shape, jnp.float32) * (3 * SP * PW) ** (-0.5)
    return jnp.repeat(copies, 2, axis=0).astype(jnp.bfloat16)


def touch_ends(entries, key, low, top_value):
    spot = [jax.random.randint(jax.random.fold_in(key, axis), (), 0, length) for axis, length in enumerate(entries.shape)]
    widest = entries.shape.index(max(entries.shape))
    neighbour = spot[:widest] + [(spot[widest] + 1) % entries.shape[widest]] + spot[widest + 1:]
    return entries.at[tuple(spot)].set(low).at[tuple(neighbour)].set(top_value)


def block_levels(key, extent, split, least, high):
    def one(dim, shards_of):
        draws = jax.random.uniform(jax.random.fold_in(jax.random.fold_in(key, 6), dim), (shards_of,), jnp.float32, least / len(split), high / len(split))
        return jnp.repeat(jnp.exp(draws), extent[dim] // shards_of).reshape((-1,) + (1,) * (len(extent) - dim - 1))

    loudness = one(*split[0])
    for cut in split[1:]:
        loudness = loudness * one(*cut)
    return loudness


def centred(own_key, dims, deviation, limit, cuts=(), kind=jnp.bfloat16):
    result = jax.random.normal(own_key, dims, jnp.float32) * deviation
    if len(cuts) > 0:
        result = block_levels(own_key, dims, cuts, -0.22, 0.18) * result
    return jnp.clip(result, min=-limit, max=limit).astype(kind)


def setup_inputs(seed: int = 0) -> dict:
    seeds = jax.random.split(jax.random.key(seed), 10)
    own_blocks = centred(seeds[0], (N_LAYER, NOWN, N_PROW, NB, CY, N_PCOL, NB), (3 * SP * PW) ** -0.5, 0.046875, ((0, 4), (2, 16), (5, 8)))
    own_pattern = touch_ends((jax.random.randint(seeds[1], (N_LAYER, NOWN, N_PROW, CY, N_PCOL), 0, 4) < 3).astype(jnp.int32), jax.random.fold_in(seeds[1], 1), 0, 1)
    own_inverse = draw_own_inverse(jax.random.fold_in(seeds[9], 71), 0)
    pair_blocks = draw_pair_blocks(jax.random.fold_in(seeds[9], 71), 0)
    pair_inverse = draw_pair_inverse(jax.random.fold_in(seeds[9], 71), 0)
    root_blocks = centred(seeds[5], (NROOT, N_PROW, NB, CY, N_PCOL, NB), (3 * SP * PW) ** -0.5, 0.046875, ((1, 16), (4, 8)))
    root_inverse = draw_root_inverse(jax.random.fold_in(seeds[9], 71), 0)
    own_rhs = centred(seeds[7], (N_LAYER, SP, N_PROW, NB, NRHS), 1.0, 6.0, ((0, 4), (2, 16)))
    shared_rhs = centred(seeds[8], (N_LAYER, 2 * SP, N_PROW, NB, NRHS), 0.5, 3.0, ((0, 4), (2, 16)))
    return dict(own_blocks=own_blocks, own_pattern=own_pattern, own_inverse=own_inverse, pair_blocks=pair_blocks, pair_inverse=pair_inverse, root_blocks=root_blocks, root_inverse=root_inverse, own_rhs=own_rhs, shared_rhs=shared_rhs)


def rounded(values):
    return lax.optimization_barrier(values.astype(jnp.bfloat16)).astype(jnp.float32)


def column_offsets(chain_length, first_col, last_col):
    offsets = []
    position = 0
    for column in range(first_col, last_col):
        offsets.append(position)
        position += chain_length - 1 - column
    return offsets


def grouped_product(factor_block, solution):
    left_side = factor_block.astype(jnp.float32).reshape(PW, CY, N_PCOL, NB)
    right_side = solution.astype(jnp.float32).reshape(CY, N_PCOL, NB, NRHS)
    return jnp.einsum("icqb,cqbr->qir", left_side, right_side)


def solve_panel(groups, base_rows, stored_inverse):
    residual = base_rows + jnp.sum(rounded(groups), axis=0)
    right_side = rounded(residual).reshape(N_PROW, NB, NRHS)
    left_side = stored_inverse.astype(jnp.float32).reshape(N_PROW, NB, PW)
    row_parts = rounded(jnp.einsum("pai,par->pir", left_side, right_side))
    return jnp.sum(row_parts, axis=0).astype(jnp.bfloat16)


def reference(own_blocks, own_pattern, own_inverse, pair_blocks, pair_inverse, root_blocks, root_inverse, own_rhs, shared_rhs):
    chain_length = 3 * SP
    own_rows = own_rhs.astype(jnp.float32).reshape(N_LAYER, SP, PW, NRHS)
    shared_rows = shared_rhs.astype(jnp.float32).reshape(N_LAYER, 2 * SP, PW, NRHS)
    own_offsets = column_offsets(chain_length, 0, SP)
    pair_offsets = column_offsets(chain_length, SP, 2 * SP)
    root_offsets = column_offsets(chain_length, 2 * SP, chain_length)
    zero_groups = jnp.zeros((N_PCOL, PW, NRHS), jnp.float32)
    first_group = (jnp.arange(N_PCOL) == 0).astype(jnp.float32).reshape(N_PCOL, 1, 1)
    own_solutions = []
    ancestor_groups = []
    for layer_index in range(N_LAYER):
        groups = [zero_groups for target in range(SP)]
        groups = groups + [first_group * shared_rows[layer_index, target] for target in range(2 * SP)]
        layer_solutions = []
        for column in range(SP):
            solution = solve_panel(groups[column], own_rows[layer_index, column], own_inverse[layer_index, column])
            layer_solutions.append(solution)
            for target in range(column + 1, chain_length):
                slot_index = own_offsets[column] + target - column - 1
                kept_tiles = (own_pattern[layer_index, slot_index] > 0)[:, None, :, :, None]
                factor_block = jnp.where(kept_tiles, own_blocks[layer_index, slot_index], jnp.zeros((), own_blocks.dtype))
                groups[target] = groups[target] - grouped_product(factor_block.reshape(PW, PW), solution)
        own_solutions.append(jnp.stack(layer_solutions))
        ancestor_groups.append(groups[SP:])
    pair_solutions = []
    root_groups = [zero_groups for target in range(SP)]
    for parent in range(N_LAYER // 2):
        inner_groups = [ancestor_groups[2 * parent][target] + ancestor_groups[2 * parent + 1][target] for target in range(2 * SP)]
        parent_solutions = []
        for column in range(SP):
            solution = solve_panel(inner_groups[column], 0.0, pair_inverse[2 * parent, column])
            parent_solutions.append(solution)
            for target in range(column + 1, 2 * SP):
                slot_index = pair_offsets[column] + target - column - 1
                factor_block = pair_blocks[2 * parent, slot_index].reshape(PW, PW)
                inner_groups[target] = inner_groups[target] - grouped_product(factor_block, solution)
        pair_solutions.append(jnp.stack(parent_solutions))
        pair_solutions.append(jnp.stack(parent_solutions))
        root_groups = [root_groups[target] + inner_groups[SP + target] for target in range(SP)]
    root_solutions = []
    for column in range(SP):
        solution = solve_panel(root_groups[column], 0.0, root_inverse[column])
        root_solutions.append(solution)
        for target in range(column + 1, SP):
            slot_index = root_offsets[column] + target - column - 1
            factor_block = root_blocks[slot_index].reshape(PW, PW)
            root_groups[target] = root_groups[target] - grouped_product(factor_block, solution)
    own_out = jnp.stack(own_solutions).reshape(N_LAYER, SP, CY, N_PCOL, NB, NRHS)
    pair_out = jnp.stack(pair_solutions).reshape(N_LAYER, SP, CY, N_PCOL, NB, NRHS)
    root_single = jnp.stack(root_solutions).reshape(SP, CY, N_PCOL, NB, NRHS)
    root_out = jnp.stack([root_single for layer_index in range(N_LAYER)])
    return own_out, pair_out, root_out
```

```python
import jax
import jax.numpy as jnp
from jax import lax
from jax.sharding import PartitionSpec as P


def from_partner(array, axis, apart):
    return lax.ppermute(array, axis, [(i, i ^ 1 << apart) for i in range(lax.axis_size(axis))])


def column_product(stacked, solved):
    block_count, row_count, col_width = stacked.shape
    flattened = stacked.reshape(block_count * row_count, col_width)
    product = jnp.dot(flattened, solved, preferred_element_type=jnp.float32)
    return product.reshape(block_count, row_count, solved.shape[1])


def shared_with_all(value, axis):
    copies = jnp.broadcast_to(value[None], (lax.axis_size(axis),) + value.shape)
    return lax.all_to_all(copies, axis, 0, 0)


def row_total(partial_value):
    partials = shared_with_all(partial_value.astype(jnp.bfloat16), "pcol")
    return jnp.sum(partials.astype(jnp.float32), axis=0)


def column_total(partial_value):
    ways = lax.axis_size("prow")
    rows, width = partial_value.shape
    pieces = partial_value.astype(jnp.bfloat16).reshape(ways, rows // ways, width)
    received = lax.all_to_all(pieces, "prow", 0, 0)
    piece = jnp.sum(received.astype(jnp.float32), axis=0).astype(jnp.bfloat16)
    return shared_with_all(piece, "prow").reshape(rows, width)


def panel_solve(residual, inverse):
    rounded = residual.astype(jnp.bfloat16)
    partial_value = lax.dot_general(
        inverse, rounded, (((0,), (0,)), ((), ())), preferred_element_type=jnp.float32
    )
    return column_total(partial_value)


def forward_solve(
    own_cols, own_inv, pair_cols, pair_inv, root_cols, root_inv, own_rows, shared_rows
):
    panels = own_inv.shape[0]
    chain_length = 3 * panels
    first_col = lax.axis_index("pcol") == 0
    solved = []
    updates_sum = jnp.zeros((chain_length,) + own_rows.shape[1:], jnp.float32)
    offset = 0
    for step_index in range(panels):
        residual = own_rows[step_index].astype(jnp.float32)
        if step_index > 0:
            residual = residual + row_total(-updates_sum[step_index])
        panel_result = panel_solve(residual, own_inv[step_index])
        solved.append(panel_result)
        block_count = chain_length - 1 - step_index
        update = column_product(own_cols[offset : offset + block_count], panel_result)
        updates_sum = updates_sum.at[step_index + 1 :].add(update)
        offset += block_count
    ancestors = jnp.where(first_col, shared_rows.astype(jnp.float32), 0.0) - updates_sum[panels:]
    ancestors = ancestors + from_partner(ancestors.astype(jnp.bfloat16), "layer", 0).astype(
        ancestors.dtype
    )
    parent_part = ancestors[:panels]
    inner_sums = jnp.zeros_like(ancestors)
    offset = 0
    for step_index in range(panels):
        residual = row_total(parent_part[step_index] - inner_sums[step_index])
        panel_result = panel_solve(residual, pair_inv[step_index])
        solved.append(panel_result)
        block_count = 2 * panels - 1 - step_index
        update = column_product(pair_cols[offset : offset + block_count], panel_result)
        inner_sums = inner_sums.at[step_index + 1 :].add(update)
        offset += block_count
    joined = ancestors[panels:] - inner_sums[panels:]
    joined = joined + from_partner(joined.astype(jnp.bfloat16), "layer", 1).astype(joined.dtype)
    root_sums = jnp.zeros_like(joined)
    offset = 0
    for step_index in range(panels):
        residual = row_total(joined[step_index] - root_sums[step_index])
        panel_result = panel_solve(residual, root_inv[step_index])
        solved.append(panel_result)
        block_count = panels - 1 - step_index
        if block_count > 0:
            update = column_product(root_cols[offset : offset + block_count], panel_result)
            root_sums = root_sums.at[step_index + 1 :].add(update)
            offset += block_count
    return solved


def local(
    own_blocks,
    own_pattern,
    own_inverse,
    pair_blocks,
    pair_inverse,
    root_blocks,
    root_inverse,
    own_rhs,
    shared_rhs,
):
    tile_rows = own_blocks.shape[3]
    cycles = own_blocks.shape[4]
    col_width = cycles * tile_rows
    rhs_width = own_rhs.shape[-1]
    own_tiles = own_blocks.reshape(-1, tile_rows, cycles, tile_rows)
    kept_tiles = own_pattern.reshape(-1, 1, cycles, 1) > 0
    own_cols = jnp.where(kept_tiles, own_tiles, jnp.zeros((), own_tiles.dtype)).reshape(
        -1, tile_rows, col_width
    )
    pair_cols = pair_blocks.reshape(-1, tile_rows, col_width)
    root_cols = root_blocks.reshape(-1, tile_rows, col_width)
    own_inv = own_inverse.reshape(-1, tile_rows, col_width)
    pair_inv = pair_inverse.reshape(-1, tile_rows, col_width)
    root_inv = root_inverse.reshape(-1, tile_rows, col_width)
    own_rows = own_rhs.reshape(-1, tile_rows, rhs_width)
    shared_rows = shared_rhs.reshape(-1, tile_rows, rhs_width)
    panels = own_inv.shape[0]
    solved = jnp.stack(
        forward_solve(
            own_cols, own_inv, pair_cols, pair_inv, root_cols, root_inv, own_rows, shared_rows
        )
    )
    solved = solved.reshape(3 * panels, cycles, 1, tile_rows, rhs_width)
    return (solved[:panels][None], solved[panels : 2 * panels][None], solved[2 * panels :][None])


def solution(mesh):
    return jax.shard_map(
        local,
        mesh=mesh,
        in_specs=(
            P("layer", None, "prow", None, None, "pcol", None),
            P("layer", None, "prow", None, "pcol"),
            P("layer", None, "prow", None, None, "pcol", None),
            P("layer", None, "prow", None, None, "pcol", None),
            P("layer", None, "prow", None, None, "pcol", None),
            P(None, "prow", None, None, "pcol", None),
            P(None, "prow", None, None, "pcol", None),
            P("layer", None, "prow", None, None),
            P("layer", None, "prow", None, None),
        ),
        out_specs=(
            P("layer", None, None, "pcol", None, None),
            P("layer", None, None, "pcol", None, None),
            P("layer", None, None, "pcol", None, None),
        ),
        check_vma=False,
    )
```

```python
import jax
import jax.numpy as jnp
from jax import lax
from jax.sharding import PartitionSpec as P


def shared_with_all(value, axis):
    copies = jnp.broadcast_to(value[None], (lax.axis_size(axis),) + value.shape)
    return lax.all_to_all(copies, axis, 0, 0)


def row_total(partial_value):
    partials = shared_with_all(partial_value.astype(jnp.bfloat16), "pcol")
    return jnp.sum(partials.astype(jnp.float32), axis=0)


def column_total(partial_value):
    ways = lax.axis_size("prow")
    rows, width = partial_value.shape
    pieces = partial_value.astype(jnp.bfloat16).reshape(ways, rows // ways, width)
    received = lax.all_to_all(pieces, "prow", 0, 0)
    piece = jnp.sum(received.astype(jnp.float32), axis=0).astype(jnp.bfloat16)
    return shared_with_all(piece, "prow").reshape(rows, width)


def sibling_groups():
    prows = lax.axis_size("prow")
    return [
        [layer * prows + p for layer in (first, first + 1) for p in range(prows)]
        for first in range(0, lax.axis_size("layer"), 2)
    ]


def among_siblings(pieces):
    return lax.all_to_all(
        pieces, ("layer", "prow"), 0, 0, axis_index_groups=sibling_groups()
    )


def own_solve(own_cols, own_inv, own_rows, shared_turned):
    panels = own_inv.shape[0]
    chain_length = 3 * panels
    solved = []
    within = [None] * panels
    beyond = jnp.where(lax.axis_index("pcol") == 0, shared_turned.astype(jnp.float32), 0.0)
    offset = 0
    for step in range(panels):
        residual = own_rows[step].astype(jnp.float32)
        if within[step] is not None:
            residual = residual - row_total(within[step])
        partial_value = lax.dot_general(
            own_inv[step],
            residual.astype(jnp.bfloat16),
            (((0,), (0,)), ((), ())),
            preferred_element_type=jnp.float32,
        )
        result = column_total(partial_value)
        solved.append(result)
        for target in range(step + 1, panels):
            update = jnp.dot(
                own_cols[offset + target - step - 1], result, preferred_element_type=jnp.float32
            )
            within[target] = update if within[target] is None else within[target] + update
        first = offset + panels - step - 1
        beyond = beyond - lax.dot_general(
            result,
            own_cols[first : first + 2 * panels],
            (((0,), (2,)), ((), ())),
            preferred_element_type=jnp.float32,
        )
        offset += chain_length - 1 - step
    return solved, beyond


def gathered_columns(inverses, blocks):
    tile_rows, cycles = blocks.shape[-4], blocks.shape[-3]
    stacked = jnp.concatenate(
        [part.reshape(-1, tile_rows, cycles * blocks.shape[-1]) for part in (inverses, blocks)]
    )
    return lax.all_gather(stacked, "prow")


def slice_solve(sums, gathered, panels):
    width, prows, targets, tile_rows = sums.shape
    sums = [sums[:, :, t] for t in range(targets)]
    solved = []
    offset = panels
    for step in range(panels):
        residual = row_total(sums[step]).astype(jnp.bfloat16)
        result = lax.dot_general(
            residual,
            gathered[:, step],
            (((1, 2), (0, 1)), ((), ())),
            preferred_element_type=jnp.float32,
        ).astype(jnp.bfloat16)
        solved.append(result)
        for target in range(step + 1, targets):
            sums[target] = sums[target] - lax.dot_general(
                result,
                gathered[:, offset + target - step - 1],
                (((1,), (2,)), ((), ())),
                preferred_element_type=jnp.float32,
            )
        offset += targets - 1 - step
    return jnp.stack(solved), sums[panels:]


def local(
    own_blocks,
    own_pattern,
    own_inverse,
    pair_blocks,
    pair_inverse,
    root_blocks,
    root_inverse,
    own_rhs,
    shared_rhs,
):
    tile_rows = own_blocks.shape[3]
    cycles = own_blocks.shape[4]
    col_width = cycles * tile_rows
    rhs_width = own_rhs.shape[-1]
    prows = lax.axis_size("prow")
    siblings = 2 * prows
    share = rhs_width // siblings
    panels = own_inverse.shape[1]
    pair_all = gathered_columns(pair_inverse, pair_blocks)
    root_all = gathered_columns(root_inverse, root_blocks)
    own_tiles = own_blocks.reshape(-1, tile_rows, cycles, tile_rows)
    kept_tiles = own_pattern.reshape(-1, 1, cycles, 1) > 0
    own_cols = jnp.where(kept_tiles, own_tiles, jnp.zeros((), own_tiles.dtype)).reshape(
        -1, tile_rows, col_width
    )
    own_inv = own_inverse.reshape(-1, tile_rows, col_width)
    own_rows = own_rhs.reshape(-1, tile_rows, rhs_width)
    shared_turned = jnp.transpose(shared_rhs.reshape(-1, tile_rows, rhs_width), (2, 0, 1))

    own_solved, beyond = own_solve(own_cols, own_inv, own_rows, shared_turned)

    pieces = beyond.astype(jnp.bfloat16).reshape(siblings, share, 2 * panels, tile_rows)
    received = among_siblings(pieces).reshape(2, prows, share, 2 * panels, tile_rows)
    sums = jnp.sum(received.astype(jnp.float32), axis=0).transpose(1, 0, 2, 3)
    pair_solved, left = slice_solve(sums, pair_all, panels)

    joined = jnp.stack(left, axis=2)
    swap = [(i, i ^ 2) for i in range(lax.axis_size("layer"))]
    joined = joined + lax.ppermute(joined.astype(jnp.bfloat16), "layer", swap).astype(joined.dtype)
    root_solved, _ = slice_solve(joined, root_all, panels)

    both = jnp.concatenate([pair_solved, root_solved])
    copies = jnp.broadcast_to(both[None], (siblings,) + both.shape)
    whole = among_siblings(copies)
    whole = whole.transpose(1, 3, 0, 2).reshape(2, 1, panels, cycles, 1, tile_rows, rhs_width)
    own_out = jnp.stack(own_solved).reshape(1, panels, cycles, 1, tile_rows, rhs_width)
    return own_out, whole[0], whole[1]


def solution(mesh):
    return jax.shard_map(
        local,
        mesh=mesh,
        in_specs=(
            P("layer", None, "prow", None, None, "pcol", None),
            P("layer", None, "prow", None, "pcol"),
            P("layer", None, "prow", None, None, "pcol", None),
            P("layer", None, "prow", None, None, "pcol", None),
            P("layer", None, "prow", None, None, "pcol", None),
            P(None, "prow", None, None, "pcol", None),
            P(None, "prow", None, None, "pcol", None),
            P("layer", None, "prow", None, None),
            P("layer", None, "prow", None, None),
        ),
        out_specs=(
            P("layer", None, None, "pcol", None, None),
            P("layer", None, None, "pcol", None, None),
            P("layer", None, None, "pcol", None, None),
        ),
        check_vma=False,
    )
```

```python
import jax
import jax.numpy as jnp
from jax import lax
from jax.sharding import PartitionSpec as P


def shared_with_all(value, axis):
    copies = jnp.broadcast_to(value[None], (lax.axis_size(axis),) + value.shape)
    return lax.all_to_all(copies, axis, 0, 0)


def row_total(partial_value):
    partials = shared_with_all(partial_value.astype(jnp.bfloat16), "pcol")
    return jnp.sum(partials.astype(jnp.float32), axis=0)


def column_total(partial_value):
    ways = lax.axis_size("prow")
    rows, width = partial_value.shape
    pieces = partial_value.astype(jnp.bfloat16).reshape(ways, rows // ways, width)
    received = lax.all_to_all(pieces, "prow", 0, 0)
    piece = jnp.sum(received.astype(jnp.float32), axis=0).astype(jnp.bfloat16)
    return shared_with_all(piece, "prow").reshape(rows, width)


def sibling_groups():
    prows = lax.axis_size("prow")
    return [
        [layer * prows + p for layer in (first, first + 1) for p in range(prows)]
        for first in range(0, lax.axis_size("layer"), 2)
    ]


def among_siblings(pieces):
    return lax.all_to_all(
        pieces, ("layer", "prow"), 0, 0, axis_index_groups=sibling_groups()
    )


def among_layers(pieces):
    return lax.all_to_all(pieces, ("layer", "prow"), 0, 0)


def own_solve(own_cols, own_inv, own_rows, shared_turned):
    panels = own_inv.shape[0]
    chain_length = 3 * panels
    solved = []
    within = [None] * panels
    beyond = jnp.where(lax.axis_index("pcol") == 0, shared_turned.astype(jnp.float32), 0.0)
    offset = 0
    for step in range(panels):
        residual = own_rows[step].astype(jnp.float32)
        if within[step] is not None:
            residual = residual - row_total(within[step])
        partial_value = lax.dot_general(
            own_inv[step],
            residual.astype(jnp.bfloat16),
            (((0,), (0,)), ((), ())),
            preferred_element_type=jnp.float32,
        )
        result = column_total(partial_value)
        solved.append(result)
        for target in range(step + 1, panels):
            update = jnp.dot(
                own_cols[offset + target - step - 1], result, preferred_element_type=jnp.float32
            )
            within[target] = update if within[target] is None else within[target] + update
        first = offset + panels - step - 1
        beyond = beyond - lax.dot_general(
            result,
            own_cols[first : first + 2 * panels],
            (((0,), (2,)), ((), ())),
            preferred_element_type=jnp.float32,
        )
        offset += chain_length - 1 - step
    return solved, beyond


def as_blocks(stored):
    tile_rows, cycles = stored.shape[-4], stored.shape[-3]
    return stored.reshape(-1, tile_rows, cycles * stored.shape[-1])


def slice_solve(sums, gathered, panels):
    sums = [sums[:, :, t] for t in range(panels)]
    solved = []
    offset = panels
    for step in range(panels):
        residual = row_total(sums[step]).astype(jnp.bfloat16)
        result = lax.dot_general(
            residual,
            gathered[:, step],
            (((1, 2), (0, 1)), ((), ())),
            preferred_element_type=jnp.float32,
        ).astype(jnp.bfloat16)
        solved.append(result)
        for target in range(step + 1, panels):
            sums[target] = sums[target] - lax.dot_general(
                result,
                gathered[:, offset + target - step - 1],
                (((1,), (2,)), ((), ())),
                preferred_element_type=jnp.float32,
            )
        offset += panels - 1 - step
    return jnp.stack(solved)


def local(
    own_blocks,
    own_pattern,
    own_inverse,
    pair_blocks,
    pair_inverse,
    root_blocks,
    root_inverse,
    own_rhs,
    shared_rhs,
):
    tile_rows = own_blocks.shape[3]
    cycles = own_blocks.shape[4]
    col_width = cycles * tile_rows
    rhs_width = own_rhs.shape[-1]
    panels = own_inverse.shape[1]
    layers, prows = lax.axis_size("layer"), lax.axis_size("prow")

    pair_cols = as_blocks(pair_blocks)
    inside, outside = [], []
    offset = 0
    for step in range(panels):
        cut = offset + panels - 1 - step
        inside.append(pair_cols[offset:cut])
        outside.append(pair_cols[cut : cut + panels])
        offset = cut + panels
    pair_all = lax.all_gather(jnp.concatenate([as_blocks(pair_inverse)] + inside), "prow")
    root_all = lax.all_gather(
        jnp.concatenate([as_blocks(root_inverse), as_blocks(root_blocks)]), "prow"
    )

    own_tiles = own_blocks.reshape(-1, tile_rows, cycles, tile_rows)
    kept_tiles = own_pattern.reshape(-1, 1, cycles, 1) > 0
    own_cols = jnp.where(kept_tiles, own_tiles, jnp.zeros((), own_tiles.dtype)).reshape(
        -1, tile_rows, col_width
    )
    own_inv = own_inverse.reshape(-1, tile_rows, col_width)
    own_rows = own_rhs.reshape(-1, tile_rows, rhs_width)
    shared_turned = jnp.transpose(shared_rhs.reshape(-1, tile_rows, rhs_width), (2, 0, 1))

    own_solved, beyond = own_solve(own_cols, own_inv, own_rows, shared_turned)

    share = rhs_width // (2 * prows)
    pieces = beyond[:, :panels].astype(jnp.bfloat16)
    received = among_siblings(pieces.reshape(2 * prows, share, panels, tile_rows))
    received = received.reshape(2, prows, share, panels, tile_rows)
    sums = jnp.sum(received.astype(jnp.float32), axis=0).transpose(1, 0, 2, 3)
    pair_solved = slice_solve(sums, pair_all, panels)
    copies = jnp.broadcast_to(pair_solved[None], (2 * prows,) + pair_solved.shape)
    pair_turned = among_siblings(copies).transpose(1, 0, 2, 3).reshape(panels, rhs_width, col_width)

    left = beyond[:, panels:]
    for step in range(panels):
        left = left - 0.5 * lax.dot_general(
            pair_turned[step],
            outside[step],
            (((1,), (2,)), ((), ())),
            preferred_element_type=jnp.float32,
        )
    share = rhs_width // (layers * prows)
    pieces = left.astype(jnp.bfloat16).reshape(layers * prows, share, panels, tile_rows)
    received = among_layers(pieces).reshape(layers, prows, share, panels, tile_rows)
    sums = jnp.sum(received.astype(jnp.float32), axis=0).transpose(1, 0, 2, 3)
    root_solved = slice_solve(sums, root_all, panels)
    by_layer = shared_with_all(shared_with_all(root_solved, "prow"), "layer")
    root_turned = by_layer.transpose(2, 0, 1, 3, 4).reshape(panels, rhs_width, col_width)

    shape = (1, panels, cycles, 1, tile_rows, rhs_width)
    return (
        jnp.stack(own_solved).reshape(shape),
        pair_turned.transpose(0, 2, 1).reshape(shape),
        root_turned.transpose(0, 2, 1).reshape(shape),
    )


def solution(mesh):
    return jax.shard_map(
        local,
        mesh=mesh,
        in_specs=(
            P("layer", None, "prow", None, None, "pcol", None),
            P("layer", None, "prow", None, "pcol"),
            P("layer", None, "prow", None, None, "pcol", None),
            P("layer", None, "prow", None, None, "pcol", None),
            P("layer", None, "prow", None, None, "pcol", None),
            P(None, "prow", None, None, "pcol", None),
            P(None, "prow", None, None, "pcol", None),
            P("layer", None, "prow", None, None),
            P("layer", None, "prow", None, None),
        ),
        out_specs=(
            P("layer", None, None, "pcol", None, None),
            P("layer", None, None, "pcol", None, None),
            P("layer", None, None, "pcol", None, None),
        ),
        check_vma=False,
    )
```

```python
import jax
import jax.numpy as jnp
from jax import lax
from jax.sharding import PartitionSpec as P


def shared_with_all(value, axis):
    copies = jnp.broadcast_to(value[None], (lax.axis_size(axis),) + value.shape)
    return lax.all_to_all(copies, axis, 0, 0)


def row_total(partial_value):
    partials = shared_with_all(partial_value.astype(jnp.bfloat16), "pcol")
    return jnp.sum(partials.astype(jnp.float32), axis=0)


def transposed_product(solved, blocks):
    return lax.dot_general(
        solved,
        blocks,
        (((solved.ndim - 1,), (blocks.ndim - 1,)), ((), ())),
        preferred_element_type=jnp.float32,
    )


def column_total(partial_value):
    ways = lax.axis_size("prow")
    rows, width = partial_value.shape
    pieces = partial_value.reshape(ways, rows // ways, width)
    received = lax.all_to_all(pieces, "prow", 0, 0)
    piece = jnp.sum(received.astype(jnp.float32), axis=0).astype(jnp.bfloat16)
    return shared_with_all(piece, "prow").reshape(rows, width)


def inverse_product(inverse, residual):
    return lax.dot_general(
        inverse,
        residual.astype(jnp.bfloat16),
        (((0,), (0,)), ((), ())),
        preferred_element_type=jnp.float32,
    ).astype(jnp.bfloat16)


def layer_swap(value, apart):
    return lax.ppermute(value, "layer", [(i, i ^ apart) for i in range(lax.axis_size("layer"))])


def as_blocks(stored):
    tile_rows, cycles = stored.shape[-4], stored.shape[-3]
    return stored.reshape(-1, tile_rows, cycles * stored.shape[-1])


def by_column(cols, panels, chain_length):
    inside, outside = [], []
    offset = 0
    for step in range(panels):
        cut = offset + panels - 1 - step
        inside.append(cols[offset:cut])
        offset += chain_length - 1 - step
        outside.append(cols[cut:offset])
    return inside, outside


def slice_solve(sums, gathered, panels):
    sums = [sums[:, :, t] for t in range(panels)]
    solved = []
    offset = panels
    for step in range(panels):
        residual = row_total(sums[step]).astype(jnp.bfloat16)
        result = lax.dot_general(
            residual,
            gathered[:, step],
            (((1, 2), (0, 1)), ((), ())),
            preferred_element_type=jnp.float32,
        ).astype(jnp.bfloat16)
        solved.append(result)
        for target in range(step + 1, panels):
            sums[target] = sums[target] - transposed_product(
                result, gathered[:, offset + target - step - 1]
            )
        offset += panels - 1 - step
    return jnp.stack(solved)


def local(
    own_blocks,
    own_pattern,
    own_inverse,
    pair_blocks,
    pair_inverse,
    root_blocks,
    root_inverse,
    own_rhs,
    shared_rhs,
):
    tile_rows = own_blocks.shape[3]
    cycles = own_blocks.shape[4]
    col_width = cycles * tile_rows
    rhs_width = own_rhs.shape[-1]
    panels = own_inverse.shape[1]
    layers, prows = lax.axis_size("layer"), lax.axis_size("prow")
    second = lax.axis_index("layer") % 2
    wide = rhs_width // prows
    half = wide // 2
    narrow = wide // layers

    own_inv = own_inverse.reshape(-1, tile_rows, col_width)
    own_rows = own_rhs.reshape(-1, tile_rows, rhs_width)
    first_partial = inverse_product(own_inv[0], own_rows[0])
    (
        first_partial,
        own_blocks,
        own_pattern,
        pair_blocks,
        pair_inverse,
        root_blocks,
        root_inverse,
        shared_rhs,
    ) = lax.optimization_barrier(
        (
            first_partial,
            own_blocks,
            own_pattern,
            pair_blocks,
            pair_inverse,
            root_blocks,
            root_inverse,
            shared_rhs,
        )
    )

    own_tiles = own_blocks.reshape(-1, tile_rows, cycles, tile_rows)
    kept_tiles = own_pattern.reshape(-1, 1, cycles, 1) > 0
    own_cols = jnp.where(kept_tiles, own_tiles, jnp.zeros((), own_tiles.dtype)).reshape(
        -1, tile_rows, col_width
    )
    own_in, own_out = by_column(own_cols, panels, 3 * panels)
    pair_in, pair_out = by_column(as_blocks(pair_blocks), panels, 2 * panels)
    pair_all = lax.all_gather(
        jnp.concatenate([as_blocks(pair_inverse)] + pair_in + [own_out[-1][:panels]]), "prow"
    )
    root_all = lax.all_gather(
        jnp.concatenate([as_blocks(root_inverse), as_blocks(root_blocks)]), "prow"
    )

    shared_turned = jnp.transpose(shared_rhs.reshape(-1, tile_rows, rhs_width), (2, 0, 1))
    beyond = jnp.where(lax.axis_index("pcol") == 0, shared_turned.astype(jnp.float32), 0.0)
    within = [None] * panels
    own_solved = []
    for step in range(panels - 1):
        if step == 0:
            partial_value = first_partial
        else:
            residual = own_rows[step].astype(jnp.float32) - row_total(within[step])
            partial_value = inverse_product(own_inv[step], residual)
        result = column_total(partial_value)
        own_solved.append(result)
        for target in range(step + 1, panels):
            block = own_in[step][target - step - 1]
            update = jnp.dot(block, result, preferred_element_type=jnp.float32)
            within[target] = update if within[target] is None else within[target] + update
        beyond = beyond - lax.dot_general(
            result, own_out[step], (((0,), (2,)), ((), ())), preferred_element_type=jnp.float32
        )

    residual = own_rows[-1].astype(jnp.float32) - row_total(within[-1])
    partial_turned = lax.dot_general(
        residual.astype(jnp.bfloat16),
        own_inv[-1],
        (((0,), (0,)), ((), ())),
        preferred_element_type=jnp.float32,
    ).astype(jnp.bfloat16)
    pieces = jnp.concatenate(
        [
            partial_turned.reshape(prows, wide, col_width),
            beyond[:, :panels].astype(jnp.bfloat16).reshape(prows, wide, panels * tile_rows),
        ],
        axis=-1,
    )
    received = lax.all_to_all(pieces, "prow", 0, 0).astype(jnp.float32)
    last_own = jnp.sum(received[:, :, :col_width], axis=0).astype(jnp.bfloat16)
    ancestors = received[:, :, col_width:].reshape(prows, wide, panels, tile_rows)
    ancestors = ancestors.transpose(1, 0, 2, 3)
    ancestors = ancestors - transposed_product(last_own, pair_all[:, -panels:])

    low, high = ancestors[:half], ancestors[half:]
    kept = jnp.where(second == 0, low, high)
    given = jnp.where(second == 0, high, low)
    sums = kept + layer_swap(given.astype(jnp.bfloat16), 1).astype(jnp.float32)
    pair_solved = slice_solve(sums, pair_all, panels)
    payload = jnp.concatenate([pair_solved.reshape(panels * half, col_width), last_own])
    everywhere = shared_with_all(payload, "prow")
    last_turned = everywhere[:, panels * half :].reshape(rhs_width, col_width)
    mine = everywhere[:, : panels * half]
    theirs = layer_swap(mine, 1)
    pair_turned = jnp.where(
        second == 0, jnp.stack([mine, theirs], axis=1), jnp.stack([theirs, mine], axis=1)
    )
    pair_turned = pair_turned.reshape(prows, 2, panels, half, col_width).transpose(2, 0, 1, 3, 4)

    left = beyond[:, panels:] - transposed_product(last_turned, own_out[-1][panels:])
    mine = mine.reshape(prows, panels, half, col_width).transpose(1, 0, 2, 3)
    mine = mine.reshape(panels, prows * half, col_width)
    taken = sum(transposed_product(mine[step], pair_out[step]) for step in range(panels))
    taken = taken.reshape(prows, 1, half, panels, tile_rows)
    is_mine = jnp.arange(2).reshape(1, 2, 1, 1, 1) == second
    left = left.reshape(prows, 2, half, panels, tile_rows) - jnp.where(is_mine, taken, 0.0)
    pieces = left.astype(jnp.bfloat16).reshape(prows, layers, narrow, panels, tile_rows)
    pieces = pieces.transpose(1, 0, 2, 3, 4).reshape(layers * prows, narrow, panels, tile_rows)
    received = lax.all_to_all(pieces, ("layer", "prow"), 0, 0)
    received = received.reshape(layers, prows, narrow, panels, tile_rows)
    sums = jnp.sum(received.astype(jnp.float32), axis=0).transpose(1, 0, 2, 3)
    root_solved = slice_solve(sums, root_all, panels)
    by_layer = shared_with_all(shared_with_all(root_solved, "prow"), "layer")
    root_turned = by_layer.transpose(2, 1, 0, 3, 4).reshape(panels, rhs_width, col_width)

    shape = (1, panels, cycles, 1, tile_rows, rhs_width)
    own_solved.append(last_turned.T)
    return (
        jnp.stack(own_solved).reshape(shape),
        pair_turned.reshape(panels, rhs_width, col_width).transpose(0, 2, 1).reshape(shape),
        root_turned.transpose(0, 2, 1).reshape(shape),
    )


def solution(mesh):
    return jax.shard_map(
        local,
        mesh=mesh,
        in_specs=(
            P("layer", None, "prow", None, None, "pcol", None),
            P("layer", None, "prow", None, "pcol"),
            P("layer", None, "prow", None, None, "pcol", None),
            P("layer", None, "prow", None, None, "pcol", None),
            P("layer", None, "prow", None, None, "pcol", None),
            P(None, "prow", None, None, "pcol", None),
            P(None, "prow", None, None, "pcol", None),
            P("layer", None, "prow", None, None),
            P("layer", None, "prow", None, None),
        ),
        out_specs=(
            P("layer", None, None, "pcol", None, None),
            P("layer", None, None, "pcol", None, None),
            P("layer", None, None, "pcol", None, None),
        ),
        check_vma=False,
    )
```

```python
import jax
import jax.numpy as jnp
from jax import lax
from jax.sharding import PartitionSpec as P


def shared_with_all(value, axis):
    copies = jnp.broadcast_to(value[None], (lax.axis_size(axis),) + value.shape)
    return lax.all_to_all(copies, axis, 0, 0)


def row_total(partial_value):
    partials = shared_with_all(partial_value.astype(jnp.bfloat16), "pcol")
    return jnp.sum(partials.astype(jnp.float32), axis=0)


def transposed_product(solved, blocks):
    return lax.dot_general(
        solved,
        blocks,
        (((solved.ndim - 1,), (blocks.ndim - 1,)), ((), ())),
        preferred_element_type=jnp.float32,
    )


def column_total(partial_value):
    ways = lax.axis_size("prow")
    rows, width = partial_value.shape
    pieces = partial_value.reshape(ways, rows // ways, width)
    received = lax.all_to_all(pieces, "prow", 0, 0)
    piece = jnp.sum(received.astype(jnp.float32), axis=0).astype(jnp.bfloat16)
    return shared_with_all(piece, "prow").reshape(rows, width)


def inverse_product(inverse, residual):
    return lax.dot_general(
        inverse,
        residual.astype(jnp.bfloat16),
        (((0,), (0,)), ((), ())),
        preferred_element_type=jnp.float32,
    ).astype(jnp.bfloat16)


def layer_swap(value, apart):
    return lax.ppermute(value, "layer", [(i, i ^ apart) for i in range(lax.axis_size("layer"))])


def as_blocks(stored):
    tile_rows, cycles = stored.shape[-4], stored.shape[-3]
    return stored.reshape(-1, tile_rows, cycles * stored.shape[-1])


def by_column(cols, panels, chain_length):
    inside, outside = [], []
    offset = 0
    for step in range(panels):
        cut = offset + panels - 1 - step
        inside.append(cols[offset:cut])
        offset += chain_length - 1 - step
        outside.append(cols[cut:offset])
    return inside, outside


def slice_solve(first, sums, gathered, panels):
    sums = [first] + sums
    solved = []
    offset = panels
    for step in range(panels):
        residual = (first if step == 0 else row_total(sums[step])).astype(jnp.bfloat16)
        result = lax.dot_general(
            residual,
            gathered[:, step],
            (((1, 2), (0, 1)), ((), ())),
            preferred_element_type=jnp.float32,
        ).astype(jnp.bfloat16)
        solved.append(result)
        for target in range(step + 1, panels):
            sums[target] = sums[target] - transposed_product(
                result, gathered[:, offset + target - step - 1]
            )
        offset += panels - 1 - step
    return jnp.stack(solved)


def local(
    own_blocks,
    own_pattern,
    own_inverse,
    pair_blocks,
    pair_inverse,
    root_blocks,
    root_inverse,
    own_rhs,
    shared_rhs,
):
    tile_rows = own_blocks.shape[3]
    cycles = own_blocks.shape[4]
    col_width = cycles * tile_rows
    rhs_width = own_rhs.shape[-1]
    panels = own_inverse.shape[1]
    layers, prows = lax.axis_size("layer"), lax.axis_size("prow")
    second = lax.axis_index("layer") % 2
    wide = rhs_width // prows
    half = wide // 2
    narrow = wide // layers

    own_rows = own_rhs.reshape(-1, tile_rows, rhs_width)
    first_inv = own_inverse[0, 0, 0].reshape(tile_rows, col_width)
    first_partial = inverse_product(first_inv, own_rows[0])
    (
        first_partial,
        own_blocks,
        own_pattern,
        own_inverse,
        pair_blocks,
        pair_inverse,
        root_blocks,
        root_inverse,
        shared_rhs,
    ) = lax.optimization_barrier(
        (
            first_partial,
            own_blocks,
            own_pattern,
            own_inverse,
            pair_blocks,
            pair_inverse,
            root_blocks,
            root_inverse,
            shared_rhs,
        )
    )

    own_inv = own_inverse.reshape(-1, tile_rows, col_width)
    own_tiles = own_blocks.reshape(-1, tile_rows, cycles, tile_rows)
    kept_tiles = own_pattern.reshape(-1, 1, cycles, 1) > 0
    own_cols = jnp.where(kept_tiles, own_tiles, jnp.zeros((), own_tiles.dtype)).reshape(
        -1, tile_rows, col_width
    )
    own_in, own_out = by_column(own_cols, panels, 3 * panels)
    ahead = slice(own_tiles.shape[0] - 2 * panels, own_tiles.shape[0] - panels)
    early_tiles = own_blocks[0, ahead, 0].reshape(-1, tile_rows, cycles, tile_rows)
    early_kept = own_pattern[0, ahead].reshape(-1, 1, cycles, 1) > 0
    early_cols = jnp.where(early_kept, early_tiles, jnp.zeros((), own_tiles.dtype)).reshape(
        -1, tile_rows, col_width
    )
    pair_in, pair_out = by_column(as_blocks(pair_blocks), panels, 2 * panels)
    pair_all = lax.all_gather(
        jnp.concatenate([as_blocks(pair_inverse)] + pair_in + [early_cols]), "prow"
    )
    root_all = lax.all_gather(
        jnp.concatenate([as_blocks(root_inverse), as_blocks(root_blocks)]), "prow"
    )

    shared_turned = jnp.transpose(shared_rhs.reshape(-1, tile_rows, rhs_width), (2, 0, 1))
    beyond = jnp.where(lax.axis_index("pcol") == 0, shared_turned.astype(jnp.float32), 0.0)
    within = [None] * panels
    own_solved = []
    for step in range(panels - 1):
        if step == 0:
            partial_value = first_partial
        else:
            residual = own_rows[step].astype(jnp.float32) - row_total(within[step])
            partial_value = inverse_product(own_inv[step], residual)
        result = column_total(partial_value)
        own_solved.append(result)
        for target in range(step + 1, panels):
            block = own_in[step][target - step - 1]
            update = jnp.dot(block, result, preferred_element_type=jnp.float32)
            within[target] = update if within[target] is None else within[target] + update
        beyond = beyond - lax.dot_general(
            result, own_out[step], (((0,), (2,)), ((), ())), preferred_element_type=jnp.float32
        )

    residual = own_rows[-1].astype(jnp.float32) - row_total(within[-1])
    partial_turned = lax.dot_general(
        residual.astype(jnp.bfloat16),
        own_inv[-1],
        (((0,), (0,)), ((), ())),
        preferred_element_type=jnp.float32,
    ).astype(jnp.bfloat16)
    pieces = jnp.concatenate(
        [
            partial_turned.reshape(prows, wide, col_width),
            beyond[:, :panels].astype(jnp.bfloat16).reshape(prows, wide, panels * tile_rows),
        ],
        axis=-1,
    )
    received = lax.all_to_all(pieces, "prow", 0, 0).astype(jnp.float32)
    last_own = jnp.sum(received[:, :, :col_width], axis=0).astype(jnp.bfloat16)
    parts = received[:, :, col_width:].reshape(prows, wide, panels, tile_rows)
    ancestors = [
        parts[:, :, t].transpose(1, 0, 2)
        - transposed_product(last_own, pair_all[:, t - panels])
        for t in range(panels)
    ]

    pcols = lax.axis_size("pcol")
    halves = ancestors[0].astype(jnp.bfloat16).reshape(2, 1, half, prows, tile_rows)
    pieces = jnp.broadcast_to(halves, (2, pcols, half, prows, tile_rows))
    groups = [
        [layer * pcols + c for layer in (low, low + 1) for c in range(pcols)]
        for low in range(0, layers, 2)
    ]
    partials = lax.all_to_all(
        pieces.reshape((2 * pcols,) + halves.shape[2:]),
        ("layer", "pcol"),
        0,
        0,
        axis_index_groups=groups,
    )
    first = jnp.sum(partials.astype(jnp.float32), axis=0)
    later = jnp.stack(ancestors[1:])
    low, high = later[:, :half], later[:, half:]
    kept = jnp.where(second == 0, low, high)
    given = jnp.where(second == 0, high, low)
    later = kept + layer_swap(given.astype(jnp.bfloat16), 1).astype(jnp.float32)
    pair_solved = slice_solve(first, list(later), pair_all, panels)
    payload = jnp.concatenate([pair_solved.reshape(panels * half, col_width), last_own])
    everywhere = shared_with_all(payload, "prow")
    last_turned = everywhere[:, panels * half :].reshape(rhs_width, col_width)
    mine = everywhere[:, : panels * half]
    theirs = layer_swap(mine, 1)
    pair_turned = jnp.where(
        second == 0, jnp.stack([mine, theirs], axis=1), jnp.stack([theirs, mine], axis=1)
    )
    pair_turned = pair_turned.reshape(prows, 2, panels, half, col_width).transpose(2, 0, 1, 3, 4)

    left = beyond[:, panels:] - transposed_product(last_turned, own_out[-1][panels:])
    mine = mine.reshape(prows, panels, half, col_width).transpose(1, 0, 2, 3)
    mine = mine.reshape(panels, prows * half, col_width)
    taken = sum(transposed_product(mine[step], pair_out[step]) for step in range(panels))
    taken = taken.reshape(prows, 1, half, panels, tile_rows)
    is_mine = jnp.arange(2).reshape(1, 2, 1, 1, 1) == second
    left = left.reshape(prows, 2, half, panels, tile_rows) - jnp.where(is_mine, taken, 0.0)
    pieces = left.astype(jnp.bfloat16).reshape(prows, layers, narrow, panels, tile_rows)
    pieces = pieces.transpose(1, 0, 2, 3, 4).reshape(layers * prows, narrow, panels, tile_rows)
    received = lax.all_to_all(pieces, ("layer", "prow"), 0, 0)
    received = received.reshape(layers, prows, narrow, panels, tile_rows)
    sums = jnp.sum(received.astype(jnp.float32), axis=0).transpose(1, 0, 2, 3)
    sums = [sums[:, :, t] for t in range(panels)]
    root_solved = slice_solve(row_total(sums[0]), sums[1:], root_all, panels)
    by_layer = shared_with_all(shared_with_all(root_solved, "prow"), "layer")
    root_turned = by_layer.transpose(2, 1, 0, 3, 4).reshape(panels, rhs_width, col_width)

    shape = (1, panels, cycles, 1, tile_rows, rhs_width)
    own_solved.append(last_turned.T)
    return (
        jnp.stack(own_solved).reshape(shape),
        pair_turned.reshape(panels, rhs_width, col_width).transpose(0, 2, 1).reshape(shape),
        root_turned.transpose(0, 2, 1).reshape(shape),
    )


def solution(mesh):
    return jax.shard_map(
        local,
        mesh=mesh,
        in_specs=(
            P("layer", None, "prow", None, None, "pcol", None),
            P("layer", None, "prow", None, "pcol"),
            P("layer", None, "prow", None, None, "pcol", None),
            P("layer", None, "prow", None, None, "pcol", None),
            P("layer", None, "prow", None, None, "pcol", None),
            P(None, "prow", None, None, "pcol", None),
            P(None, "prow", None, None, "pcol", None),
            P("layer", None, "prow", None, None),
            P("layer", None, "prow", None, None),
        ),
        out_specs=(
            P("layer", None, None, "pcol", None, None),
            P("layer", None, None, "pcol", None, None),
            P("layer", None, None, "pcol", None, None),
        ),
        check_vma=False,
    )
```

```python
import functools

import jax
import jax.numpy as jnp
from jax import lax
from jax.experimental import pallas as pl
from jax.experimental.pallas import tpu as pltpu
from jax.sharding import PartitionSpec as P

VMEM = pl.BlockSpec(memory_space=pltpu.VMEM)
ANY = pl.BlockSpec(memory_space=pl.ANY)


def shared_with_all(value, axis):
    copies = jnp.broadcast_to(value[None], (lax.axis_size(axis),) + value.shape)
    return lax.all_to_all(copies, axis, 0, 0)


def row_total(partial_value):
    partials = shared_with_all(partial_value.astype(jnp.bfloat16), "pcol")
    return jnp.sum(partials.astype(jnp.float32), axis=0)


def transposed_product(solved, blocks):
    return lax.dot_general(
        solved,
        blocks,
        (((solved.ndim - 1,), (blocks.ndim - 1,)), ((), ())),
        preferred_element_type=jnp.float32,
    )


def column_total(partial_value):
    ways = lax.axis_size("prow")
    rows, width = partial_value.shape
    pieces = partial_value.reshape(ways, rows // ways, width)
    received = lax.all_to_all(pieces, "prow", 0, 0)
    piece = jnp.sum(received.astype(jnp.float32), axis=0).astype(jnp.bfloat16)
    return shared_with_all(piece, "prow").reshape(rows, width)


def inverse_product(inverse, residual):
    return lax.dot_general(
        inverse,
        residual.astype(jnp.bfloat16),
        (((0,), (0,)), ((), ())),
        preferred_element_type=jnp.float32,
    ).astype(jnp.bfloat16)


def layer_swap(value, apart):
    return lax.ppermute(value, "layer", [(i, i ^ apart) for i in range(lax.axis_size("layer"))])


def as_blocks(stored):
    tile_rows, cycles = stored.shape[-4], stored.shape[-3]
    return stored.reshape(-1, tile_rows, cycles * stored.shape[-1])


def by_column(cols, panels, chain_length):
    inside, outside = [], []
    offset = 0
    for step in range(panels):
        cut = offset + panels - 1 - step
        inside.append(cols[offset:cut])
        offset += chain_length - 1 - step
        outside.append(cols[cut:offset])
    return inside, outside


def as_rows(tiles):
    return tiles.reshape(tiles.shape[0] * tiles.shape[1], tiles.shape[2])


def times_rows(solved, tiles):
    return lax.dot_general(
        solved, as_rows(tiles), (((1,), (1,)), ((), ())), preferred_element_type=jnp.float32
    )


def fetch(gathered, block, buffer, arrived):
    copies = []
    for p in range(buffer.shape[0]):
        copies.append(
            pltpu.make_async_copy(gathered.at[p, block], buffer.at[p], arrived.at[p])
        )
        copies[-1].start()
    return copies


def wait_all(copies):
    for copy in copies:
        copy.wait()


def total_of(received):
    total = received[0].astype(jnp.float32)
    for w in range(1, received.shape[0]):
        total = total + received[w].astype(jnp.float32)
    return total


def step_kernel(panel, block, received, gathered, sums, solved, copies, inverse, tiles, first, then):
    stored = fetch(gathered, panel, inverse, first)
    wanted = fetch(gathered, block, tiles, then)
    total = total_of(received).astype(jnp.bfloat16)
    wait_all(stored)
    result = jnp.dot(total, as_rows(inverse[...]), preferred_element_type=jnp.float32)
    result = result.astype(jnp.bfloat16)
    solved[...] = result
    wait_all(wanted)
    left = (sums[...] - times_rows(result, tiles[...])).astype(jnp.bfloat16)
    for w in range(copies.shape[0]):
        copies[w] = left


def last_kernel(panel, received, gathered, solved, inverse, first):
    stored = fetch(gathered, panel, inverse, first)
    total = total_of(received).astype(jnp.bfloat16)
    wait_all(stored)
    result = jnp.dot(total, as_rows(inverse[...]), preferred_element_type=jnp.float32)
    solved[...] = result.astype(jnp.bfloat16)


def update_kernel(block, solved, gathered, sums, left, tiles, then):
    wait_all(fetch(gathered, block, tiles, then))
    left[...] = sums[...] - times_rows(solved[...], tiles[...])


def take_off(received, product, target, line):
    ways, _, width = received.shape
    tile_rows = product.shape[1] // ways
    start = width - (3 - target) * tile_rows
    for p in range(ways):
        here = slice(p * tile_rows, (p + 1) * tile_rows)
        part = received[p, :, start : start + tile_rows].astype(jnp.float32)
        line[:, here] = part - product[:, here]


def open_kernel(block, received, gathered, solved, copies, tiles, line, then):
    wanted = fetch(gathered, block, tiles, then)
    total = received[0, :, : solved.shape[1]].astype(jnp.float32)
    for w in range(1, received.shape[0]):
        total = total + received[w, :, : solved.shape[1]].astype(jnp.float32)
    result = total.astype(jnp.bfloat16)
    solved[...] = result
    wait_all(wanted)
    take_off(received, times_rows(result, tiles[...]), 0, line)
    half = copies.shape[1]
    for h in range(2):
        part = line[h * half : (h + 1) * half, :].astype(jnp.bfloat16)
        for w in range(copies.shape[0] // 2):
            copies[h * (copies.shape[0] // 2) + w] = part


def later_kernel(block, received, solved, gathered, sums, tiles, more, line, first, then):
    wanted = fetch(gathered, block, tiles, first)
    beside = fetch(gathered, block + 1, more, then)
    wait_all(wanted)
    take_off(received, times_rows(solved[...], tiles[...]), 1, line)
    sums[0] = line[...]
    wait_all(beside)
    take_off(received, times_rows(solved[...], more[...]), 2, line)
    sums[1] = line[...]


def call(kernel, shapes, specs, buffers, blocks, columns, gathered, *operands):
    tile = gathered.shape[:1] + gathered.shape[2:]
    size = tile[0] * tile[1] * tile[2]
    scratch = [pltpu.VMEM(tile, jnp.bfloat16)] * blocks + buffers
    scratch += [pltpu.SemaphoreType.DMA((tile[0],))] * blocks
    return pl.pallas_call(
        kernel,
        out_shape=shapes,
        in_specs=specs,
        out_specs=tuple(VMEM for _ in shapes) if isinstance(shapes, tuple) else VMEM,
        scratch_shapes=scratch,
        compiler_params=pltpu.CompilerParams(vmem_limit_bytes=59 * 2**20),
        cost_estimate=pl.CostEstimate(
            flops=2 * columns * size * blocks, bytes_accessed=2 * size * blocks, transcendentals=0
        ),
    )(*operands)


def slice_solve(received, sums, gathered, panels):
    columns, rows = received.shape[1:]
    col_width = gathered.shape[-1]
    ways = lax.axis_size("pcol")
    solved_shape = jax.ShapeDtypeStruct((columns, col_width), jnp.bfloat16)
    copies_shape = jax.ShapeDtypeStruct((ways, columns, rows), jnp.bfloat16)
    sums_shape = jax.ShapeDtypeStruct((columns, rows), jnp.float32)
    sums = [None] + list(sums)
    solved = []
    offset = panels
    for step in range(panels - 1):
        result, copies = call(
            functools.partial(step_kernel, step, offset),
            (solved_shape, copies_shape),
            [VMEM, ANY, VMEM],
            [],
            2,
            columns,
            gathered,
            received,
            gathered,
            sums[step + 1],
        )
        solved.append(result)
        received = lax.all_to_all(copies, "pcol", 0, 0)
        for target in range(step + 2, panels):
            sums[target] = call(
                functools.partial(update_kernel, offset + target - step - 1),
                sums_shape,
                [VMEM, ANY, VMEM],
                [],
                1,
                columns,
                gathered,
                result,
                gathered,
                sums[target],
            )
        offset += panels - 1 - step
    result = call(
        functools.partial(last_kernel, panels - 1),
        solved_shape,
        [VMEM, ANY],
        [],
        1,
        columns,
        gathered,
        received,
        gathered,
    )
    solved.append(result)
    return jnp.stack(solved)


def local(
    own_blocks,
    own_pattern,
    own_inverse,
    pair_blocks,
    pair_inverse,
    root_blocks,
    root_inverse,
    own_rhs,
    shared_rhs,
):
    tile_rows = own_blocks.shape[3]
    cycles = own_blocks.shape[4]
    col_width = cycles * tile_rows
    rhs_width = own_rhs.shape[-1]
    panels = own_inverse.shape[1]
    layers, prows = lax.axis_size("layer"), lax.axis_size("prow")
    second = lax.axis_index("layer") % 2
    wide = rhs_width // prows
    half = wide // 2
    narrow = wide // layers

    own_rows = own_rhs.reshape(-1, tile_rows, rhs_width)
    first_inv = own_inverse[0, 0, 0].reshape(tile_rows, col_width)
    first_partial = inverse_product(first_inv, own_rows[0])
    (
        first_partial,
        own_blocks,
        own_pattern,
        own_inverse,
        pair_blocks,
        pair_inverse,
        root_blocks,
        root_inverse,
        shared_rhs,
    ) = lax.optimization_barrier(
        (
            first_partial,
            own_blocks,
            own_pattern,
            own_inverse,
            pair_blocks,
            pair_inverse,
            root_blocks,
            root_inverse,
            shared_rhs,
        )
    )

    own_inv = own_inverse.reshape(-1, tile_rows, col_width)
    own_tiles = own_blocks.reshape(-1, tile_rows, cycles, tile_rows)
    kept_tiles = own_pattern.reshape(-1, 1, cycles, 1) > 0
    own_cols = jnp.where(kept_tiles, own_tiles, jnp.zeros((), own_tiles.dtype)).reshape(
        -1, tile_rows, col_width
    )
    own_in, own_out = by_column(own_cols, panels, 3 * panels)
    ahead = slice(own_tiles.shape[0] - 2 * panels, own_tiles.shape[0] - panels)
    early_tiles = own_blocks[0, ahead, 0].reshape(-1, tile_rows, cycles, tile_rows)
    early_kept = own_pattern[0, ahead].reshape(-1, 1, cycles, 1) > 0
    early_tiles = jnp.where(early_kept, early_tiles, jnp.zeros((), own_tiles.dtype))
    _, pair_out = by_column(as_blocks(pair_blocks), panels, 2 * panels)
    pair_tiles = pair_blocks[0, :, 0].reshape(-1, tile_rows, cycles, tile_rows)
    tiles_in, _ = by_column(pair_tiles, panels, 2 * panels)
    first_tiles = pair_inverse.reshape(-1, tile_rows, cycles, tile_rows)
    ready = lax.optimization_barrier(jnp.concatenate([first_tiles] + tiles_in + [early_tiles]))
    pair_all = lax.all_gather(ready.reshape(-1, tile_rows, col_width), "prow")
    root_all = lax.all_gather(
        jnp.concatenate([as_blocks(root_inverse), as_blocks(root_blocks)]), "prow"
    )

    shared_turned = jnp.transpose(shared_rhs.reshape(-1, tile_rows, rhs_width), (2, 0, 1))
    beyond = jnp.where(lax.axis_index("pcol") == 0, shared_turned.astype(jnp.float32), 0.0)
    within = [None] * panels
    own_solved = []
    for step in range(panels - 1):
        if step == 0:
            partial_value = first_partial
        else:
            residual = own_rows[step].astype(jnp.float32) - row_total(within[step])
            partial_value = inverse_product(own_inv[step], residual)
        result = column_total(partial_value)
        own_solved.append(result)
        for target in range(step + 1, panels):
            block = own_in[step][target - step - 1]
            update = jnp.dot(block, result, preferred_element_type=jnp.float32)
            within[target] = update if within[target] is None else within[target] + update
        beyond = beyond - lax.dot_general(
            result, own_out[step], (((0,), (2,)), ((), ())), preferred_element_type=jnp.float32
        )

    residual = own_rows[-1].astype(jnp.float32) - row_total(within[-1])
    partial_turned = lax.dot_general(
        residual.astype(jnp.bfloat16),
        own_inv[-1],
        (((0,), (0,)), ((), ())),
        preferred_element_type=jnp.float32,
    ).astype(jnp.bfloat16)
    pieces = jnp.concatenate(
        [
            partial_turned.reshape(prows, wide, col_width),
            beyond[:, :panels].astype(jnp.bfloat16).reshape(prows, wide, panels * tile_rows),
        ],
        axis=-1,
    )
    received = lax.all_to_all(pieces, "prow", 0, 0)
    pcols = lax.axis_size("pcol")
    rows = prows * tile_rows
    count = pair_all.shape[1]
    line = pltpu.VMEM((wide, rows), jnp.float32)
    last_own, copies = call(
        functools.partial(open_kernel, count - panels),
        (
            jax.ShapeDtypeStruct((wide, col_width), jnp.bfloat16),
            jax.ShapeDtypeStruct((2 * pcols, half, rows), jnp.bfloat16),
        ),
        [VMEM, ANY],
        [line],
        1,
        wide,
        pair_all,
        received,
        pair_all,
    )

    groups = [
        [layer * pcols + c for layer in (low, low + 1) for c in range(pcols)]
        for low in range(0, layers, 2)
    ]
    partials = lax.all_to_all(copies, ("layer", "pcol"), 0, 0, axis_index_groups=groups)
    later = call(
        functools.partial(later_kernel, count - panels + 1),
        jax.ShapeDtypeStruct((panels - 1, wide, rows), jnp.float32),
        [VMEM, VMEM, ANY],
        [line],
        2,
        wide,
        pair_all,
        received,
        last_own,
        pair_all,
    )
    low, high = later[:, :half], later[:, half:]
    kept = jnp.where(second == 0, low, high)
    given = jnp.where(second == 0, high, low)
    later = kept + layer_swap(given.astype(jnp.bfloat16), 1).astype(jnp.float32)
    pair_solved = slice_solve(partials, list(later), pair_all, panels)
    payload = jnp.concatenate([pair_solved.reshape(panels * half, col_width), last_own])
    everywhere = shared_with_all(payload, "prow")
    last_turned = everywhere[:, panels * half :].reshape(rhs_width, col_width)
    mine = everywhere[:, : panels * half]
    theirs = layer_swap(mine, 1)
    pair_turned = jnp.where(
        second == 0, jnp.stack([mine, theirs], axis=1), jnp.stack([theirs, mine], axis=1)
    )
    pair_turned = pair_turned.reshape(prows, 2, panels, half, col_width).transpose(2, 0, 1, 3, 4)

    left = beyond[:, panels:] - transposed_product(last_turned, own_out[-1][panels:])
    mine = mine.reshape(prows, panels, half, col_width).transpose(1, 0, 2, 3)
    mine = mine.reshape(panels, prows * half, col_width)
    taken = sum(transposed_product(mine[step], pair_out[step]) for step in range(panels))
    taken = taken.reshape(prows, 1, half, panels, tile_rows)
    is_mine = jnp.arange(2).reshape(1, 2, 1, 1, 1) == second
    left = left.reshape(prows, 2, half, panels, tile_rows) - jnp.where(is_mine, taken, 0.0)
    pieces = left.astype(jnp.bfloat16).reshape(prows, layers, narrow, panels, tile_rows)
    pieces = pieces.transpose(1, 0, 2, 3, 4).reshape(layers * prows, narrow, panels, tile_rows)
    received = lax.all_to_all(pieces, ("layer", "prow"), 0, 0)
    received = received.reshape(layers, prows, narrow, panels, tile_rows)
    sums = jnp.sum(received.astype(jnp.float32), axis=0).transpose(2, 1, 0, 3)
    sums = sums.reshape(panels, narrow, rows)
    received = shared_with_all(sums[0].astype(jnp.bfloat16), "pcol")
    root_solved = slice_solve(received, list(sums[1:]), root_all, panels)
    by_layer = shared_with_all(shared_with_all(root_solved, "prow"), "layer")
    root_turned = by_layer.transpose(2, 1, 0, 3, 4).reshape(panels, rhs_width, col_width)

    shape = (1, panels, cycles, 1, tile_rows, rhs_width)
    own_solved.append(last_turned.T)
    return (
        jnp.stack(own_solved).reshape(shape),
        pair_turned.reshape(panels, rhs_width, col_width).transpose(0, 2, 1).reshape(shape),
        root_turned.transpose(0, 2, 1).reshape(shape),
    )


def solution(mesh):
    return jax.shard_map(
        local,
        mesh=mesh,
        in_specs=(
            P("layer", None, "prow", None, None, "pcol", None),
            P("layer", None, "prow", None, "pcol"),
            P("layer", None, "prow", None, None, "pcol", None),
            P("layer", None, "prow", None, None, "pcol", None),
            P("layer", None, "prow", None, None, "pcol", None),
            P(None, "prow", None, None, "pcol", None),
            P(None, "prow", None, None, "pcol", None),
            P("layer", None, "prow", None, None),
            P("layer", None, "prow", None, None),
        ),
        out_specs=(
            P("layer", None, None, "pcol", None, None),
            P("layer", None, None, "pcol", None, None),
            P("layer", None, None, "pcol", None, None),
        ),
        check_vma=False,
    )
```

```python
import jax
import jax.numpy as jnp
from jax import lax
from jax.sharding import PartitionSpec as P


def shared_with_all(value, axis):
    copies = jnp.broadcast_to(value[None], (lax.axis_size(axis),) + value.shape)
    return lax.all_to_all(copies, axis, 0, 0)


def row_total(partial_value):
    partials = shared_with_all(partial_value.astype(jnp.bfloat16), "pcol")
    return jnp.sum(partials.astype(jnp.float32), axis=0)


def transposed_product(solved, blocks):
    return lax.dot_general(
        solved,
        blocks,
        (((solved.ndim - 1,), (blocks.ndim - 1,)), ((), ())),
        preferred_element_type=jnp.float32,
    )


def column_total(partial_value):
    ways = lax.axis_size("prow")
    rows, width = partial_value.shape
    pieces = partial_value.reshape(ways, rows // ways, width)
    received = lax.all_to_all(pieces, "prow", 0, 0)
    piece = jnp.sum(received.astype(jnp.float32), axis=0).astype(jnp.bfloat16)
    return shared_with_all(piece, "prow").reshape(rows, width)


def inverse_product(inverse, residual):
    return lax.dot_general(
        inverse,
        residual.astype(jnp.bfloat16),
        (((0,), (0,)), ((), ())),
        preferred_element_type=jnp.float32,
    ).astype(jnp.bfloat16)


def layer_swap(value, apart):
    return lax.ppermute(value, "layer", [(i, i ^ apart) for i in range(lax.axis_size("layer"))])


def as_blocks(stored):
    tile_rows, cycles = stored.shape[-4], stored.shape[-3]
    return stored.reshape(-1, tile_rows, cycles * stored.shape[-1])


def by_column(cols, panels, chain_length):
    inside, outside = [], []
    offset = 0
    for step in range(panels):
        cut = offset + panels - 1 - step
        inside.append(cols[offset:cut])
        offset += chain_length - 1 - step
        outside.append(cols[cut:offset])
    return inside, outside


def slice_solve(first, sums, gathered, panels):
    sums = [first] + sums
    solved = []
    offset = panels
    for step in range(panels):
        residual = (first if step == 0 else row_total(sums[step])).astype(jnp.bfloat16)
        result = lax.dot_general(
            residual,
            gathered[:, step],
            (((1, 2), (0, 1)), ((), ())),
            preferred_element_type=jnp.float32,
        ).astype(jnp.bfloat16)
        solved.append(result)
        for target in range(step + 1, panels):
            sums[target] = sums[target] - transposed_product(
                result, gathered[:, offset + target - step - 1]
            )
        offset += panels - 1 - step
    return jnp.stack(solved)


def local(
    own_blocks,
    own_pattern,
    own_inverse,
    pair_blocks,
    pair_inverse,
    root_blocks,
    root_inverse,
    own_rhs,
    shared_rhs,
):
    tile_rows = own_blocks.shape[3]
    cycles = own_blocks.shape[4]
    col_width = cycles * tile_rows
    rhs_width = own_rhs.shape[-1]
    panels = own_inverse.shape[1]
    layers, prows = lax.axis_size("layer"), lax.axis_size("prow")
    second = lax.axis_index("layer") % 2
    wide = rhs_width // prows
    half = wide // 2
    narrow = wide // layers

    own_rows = own_rhs.reshape(-1, tile_rows, rhs_width)
    first_inv = own_inverse[0, 0, 0].reshape(tile_rows, col_width)
    first_partial = inverse_product(first_inv, own_rows[0])
    (
        first_partial,
        own_blocks,
        own_pattern,
        own_inverse,
        pair_blocks,
        pair_inverse,
        root_blocks,
        root_inverse,
        shared_rhs,
    ) = lax.optimization_barrier(
        (
            first_partial,
            own_blocks,
            own_pattern,
            own_inverse,
            pair_blocks,
            pair_inverse,
            root_blocks,
            root_inverse,
            shared_rhs,
        )
    )

    own_inv = own_inverse.reshape(-1, tile_rows, col_width)
    own_tiles = own_blocks.reshape(-1, tile_rows, cycles, tile_rows)
    kept_tiles = own_pattern.reshape(-1, 1, cycles, 1) > 0
    own_cols = jnp.where(kept_tiles, own_tiles, jnp.zeros((), own_tiles.dtype)).reshape(
        -1, tile_rows, col_width
    )
    own_in, own_out = by_column(own_cols, panels, 3 * panels)
    ahead = slice(own_tiles.shape[0] - 2 * panels, own_tiles.shape[0] - panels)
    early_tiles = own_blocks[0, ahead, 0].reshape(-1, tile_rows, cycles, tile_rows)
    early_kept = own_pattern[0, ahead].reshape(-1, 1, cycles, 1) > 0
    early_cols = jnp.where(early_kept, early_tiles, jnp.zeros((), own_tiles.dtype)).reshape(
        -1, tile_rows, col_width
    )
    pair_in, pair_out = by_column(as_blocks(pair_blocks), panels, 2 * panels)
    pair_all = lax.all_gather(
        jnp.concatenate([as_blocks(pair_inverse)] + pair_in + [early_cols]), "prow"
    )
    root_all = lax.all_gather(
        jnp.concatenate([as_blocks(root_inverse), as_blocks(root_blocks)]), "prow"
    )

    shared_turned = jnp.transpose(shared_rhs.reshape(-1, tile_rows, rhs_width), (2, 0, 1))
    beyond = jnp.where(lax.axis_index("pcol") == 0, shared_turned.astype(jnp.float32), 0.0)
    within = [None] * panels
    own_solved = []
    for step in range(panels - 1):
        if step == 0:
            partial_value = first_partial
        else:
            residual = own_rows[step].astype(jnp.float32) - row_total(within[step])
            partial_value = inverse_product(own_inv[step], residual)
        result = column_total(partial_value)
        own_solved.append(result)
        for target in range(step + 1, panels):
            block = own_in[step][target - step - 1]
            update = jnp.dot(block, result, preferred_element_type=jnp.float32)
            within[target] = update if within[target] is None else within[target] + update
        beyond = beyond - lax.dot_general(
            result, own_out[step], (((0,), (2,)), ((), ())), preferred_element_type=jnp.float32
        )

    residual = own_rows[-1].astype(jnp.float32) - row_total(within[-1])
    partial_turned = lax.dot_general(
        residual.astype(jnp.bfloat16),
        own_inv[-1],
        (((0,), (0,)), ((), ())),
        preferred_element_type=jnp.float32,
    ).astype(jnp.bfloat16)
    pieces = jnp.concatenate(
        [
            partial_turned.reshape(prows, wide, col_width),
            beyond[:, :panels].astype(jnp.bfloat16).reshape(prows, wide, panels * tile_rows),
        ],
        axis=-1,
    )
    received = lax.all_to_all(pieces, "prow", 0, 0)
    last_own = jnp.sum(received[:, :, :col_width].astype(jnp.float32), axis=0).astype(jnp.bfloat16)
    ancestors = []
    for t in range(panels):
        start = col_width + t * tile_rows
        part = received[:, :, start : start + tile_rows].transpose(1, 0, 2)
        product = transposed_product(last_own, pair_all[:, t - panels])
        ancestors.append(part.astype(jnp.float32) - product)

    pcols = lax.axis_size("pcol")
    halves = ancestors[0].astype(jnp.bfloat16).reshape(2, 1, half, prows, tile_rows)
    pieces = jnp.broadcast_to(halves, (2, pcols, half, prows, tile_rows))
    groups = [
        [layer * pcols + c for layer in (low, low + 1) for c in range(pcols)]
        for low in range(0, layers, 2)
    ]
    partials = lax.all_to_all(
        pieces.reshape((2 * pcols,) + halves.shape[2:]),
        ("layer", "pcol"),
        0,
        0,
        axis_index_groups=groups,
    )
    first = jnp.sum(partials.astype(jnp.float32), axis=0)
    later = jnp.stack(ancestors[1:])
    low, high = later[:, :half], later[:, half:]
    kept = jnp.where(second == 0, low, high)
    given = jnp.where(second == 0, high, low)
    later = kept + layer_swap(given.astype(jnp.bfloat16), 1).astype(jnp.float32)
    pair_solved = slice_solve(first, list(later), pair_all, panels)
    payload = jnp.concatenate([pair_solved.reshape(panels * half, col_width), last_own])
    everywhere = shared_with_all(payload, "prow")
    last_turned = everywhere[:, panels * half :].reshape(rhs_width, col_width)
    mine = everywhere[:, : panels * half]
    theirs = layer_swap(mine, 1)
    pair_turned = jnp.where(
        second == 0, jnp.stack([mine, theirs], axis=1), jnp.stack([theirs, mine], axis=1)
    )
    pair_turned = pair_turned.reshape(prows, 2, panels, half, col_width).transpose(2, 0, 1, 3, 4)

    left = beyond[:, panels:] - transposed_product(last_turned, own_out[-1][panels:])
    mine = mine.reshape(prows, panels, half, col_width).transpose(1, 0, 2, 3)
    mine = mine.reshape(panels, prows * half, col_width)
    taken = sum(transposed_product(mine[step], pair_out[step]) for step in range(panels))
    taken = taken.reshape(prows, 1, half, panels, tile_rows)
    is_mine = jnp.arange(2).reshape(1, 2, 1, 1, 1) == second
    left = left.reshape(prows, 2, half, panels, tile_rows) - jnp.where(is_mine, taken, 0.0)
    pieces = left.astype(jnp.bfloat16).reshape(prows, layers, narrow, panels, tile_rows)
    pieces = pieces.transpose(1, 0, 2, 3, 4).reshape(layers * prows, narrow, panels, tile_rows)
    received = lax.all_to_all(pieces, ("layer", "prow"), 0, 0)
    received = received.reshape(layers, prows, narrow, panels, tile_rows)
    sums = jnp.sum(received.astype(jnp.float32), axis=0).transpose(1, 0, 2, 3)
    sums = [sums[:, :, t] for t in range(panels)]
    root_solved = slice_solve(row_total(sums[0]), sums[1:], root_all, panels)
    by_layer = shared_with_all(shared_with_all(root_solved, "prow"), "layer")
    root_turned = by_layer.transpose(2, 1, 0, 3, 4).reshape(panels, rhs_width, col_width)

    shape = (1, panels, cycles, 1, tile_rows, rhs_width)
    own_solved.append(last_turned.T)
    return (
        jnp.stack(own_solved).reshape(shape),
        pair_turned.reshape(panels, rhs_width, col_width).transpose(0, 2, 1).reshape(shape),
        root_turned.transpose(0, 2, 1).reshape(shape),
    )


def solution(mesh):
    return jax.shard_map(
        local,
        mesh=mesh,
        in_specs=(
            P("layer", None, "prow", None, None, "pcol", None),
            P("layer", None, "prow", None, "pcol"),
            P("layer", None, "prow", None, None, "pcol", None),
            P("layer", None, "prow", None, None, "pcol", None),
            P("layer", None, "prow", None, None, "pcol", None),
            P(None, "prow", None, None, "pcol", None),
            P(None, "prow", None, None, "pcol", None),
            P("layer", None, "prow", None, None),
            P("layer", None, "prow", None, None),
        ),
        out_specs=(
            P("layer", None, None, "pcol", None, None),
            P("layer", None, None, "pcol", None, None),
            P("layer", None, None, "pcol", None, None),
        ),
        check_vma=False,
    )
```

```python
import jax
import jax.numpy as jnp
from jax import lax
from jax.sharding import PartitionSpec as P


def shared_with_all(value, axis):
    copies = jnp.broadcast_to(value[None], (lax.axis_size(axis),) + value.shape)
    return lax.all_to_all(copies, axis, 0, 0)


def row_total(partial_value):
    partials = shared_with_all(partial_value.astype(jnp.bfloat16), "pcol")
    return jnp.sum(partials.astype(jnp.float32), axis=0)


def transposed_product(solved, blocks):
    return lax.dot_general(
        solved,
        blocks,
        (((solved.ndim - 1,), (blocks.ndim - 1,)), ((), ())),
        preferred_element_type=jnp.float32,
    )


def column_total(partial_value):
    ways = lax.axis_size("prow")
    rows, width = partial_value.shape
    pieces = partial_value.reshape(ways, rows // ways, width)
    received = lax.all_to_all(pieces, "prow", 0, 0)
    piece = jnp.sum(received.astype(jnp.float32), axis=0).astype(jnp.bfloat16)
    return shared_with_all(piece, "prow").reshape(rows, width)


def inverse_product(inverse, residual):
    return lax.dot_general(
        inverse,
        residual.astype(jnp.bfloat16),
        (((0,), (0,)), ((), ())),
        preferred_element_type=jnp.float32,
    ).astype(jnp.bfloat16)


def layer_swap(value, apart):
    return lax.ppermute(value, "layer", [(i, i ^ apart) for i in range(lax.axis_size("layer"))])


def as_blocks(stored):
    tile_rows, cycles = stored.shape[-4], stored.shape[-3]
    return stored.reshape(-1, tile_rows, cycles * stored.shape[-1])


def by_column(cols, panels, chain_length):
    inside, outside = [], []
    offset = 0
    for step in range(panels):
        cut = offset + panels - 1 - step
        inside.append(cols[offset:cut])
        offset += chain_length - 1 - step
        outside.append(cols[cut:offset])
    return inside, outside


def slice_solve(first, sums, gathered, panels):
    sums = [first] + sums
    solved = []
    offset = panels
    for step in range(panels):
        residual = (first if step == 0 else row_total(sums[step])).astype(jnp.bfloat16)
        result = lax.dot_general(
            residual,
            gathered[:, step],
            (((1, 2), (0, 1)), ((), ())),
            preferred_element_type=jnp.float32,
        ).astype(jnp.bfloat16)
        solved.append(result)
        for target in range(step + 1, panels):
            sums[target] = sums[target] - transposed_product(
                result, gathered[:, offset + target - step - 1]
            )
        offset += panels - 1 - step
    return jnp.stack(solved)


def local(
    own_blocks,
    own_pattern,
    own_inverse,
    pair_blocks,
    pair_inverse,
    root_blocks,
    root_inverse,
    own_rhs,
    shared_rhs,
):
    tile_rows = own_blocks.shape[3]
    cycles = own_blocks.shape[4]
    col_width = cycles * tile_rows
    rhs_width = own_rhs.shape[-1]
    panels = own_inverse.shape[1]
    layers, prows = lax.axis_size("layer"), lax.axis_size("prow")
    second = lax.axis_index("layer") % 2
    wide = rhs_width // prows
    half = wide // 2
    narrow = wide // layers

    own_rows = own_rhs.reshape(-1, tile_rows, rhs_width)
    first_inv = own_inverse[0, 0, 0].reshape(tile_rows, col_width)
    first_partial = inverse_product(first_inv, own_rows[0])
    (
        first_partial,
        own_blocks,
        own_pattern,
        own_inverse,
        pair_blocks,
        pair_inverse,
        root_blocks,
        root_inverse,
        shared_rhs,
    ) = lax.optimization_barrier(
        (
            first_partial,
            own_blocks,
            own_pattern,
            own_inverse,
            pair_blocks,
            pair_inverse,
            root_blocks,
            root_inverse,
            shared_rhs,
        )
    )

    own_inv = own_inverse.reshape(-1, tile_rows, col_width)
    own_tiles = own_blocks.reshape(-1, tile_rows, cycles, tile_rows)
    kept_tiles = own_pattern.reshape(-1, 1, cycles, 1) > 0
    own_cols = jnp.where(kept_tiles, own_tiles, jnp.zeros((), own_tiles.dtype)).reshape(
        -1, tile_rows, col_width
    )
    own_in, own_out = by_column(own_cols, panels, 3 * panels)
    ahead = slice(own_tiles.shape[0] - 2 * panels, own_tiles.shape[0] - panels)
    early_tiles = own_blocks[0, ahead, 0].reshape(-1, tile_rows, cycles, tile_rows)
    early_kept = own_pattern[0, ahead].reshape(-1, 1, cycles, 1) > 0
    early_cols = jnp.where(early_kept, early_tiles, jnp.zeros((), own_tiles.dtype)).reshape(
        -1, tile_rows, col_width
    )
    pair_in, pair_out = by_column(as_blocks(pair_blocks), panels, 2 * panels)
    pair_all = lax.all_gather(
        jnp.concatenate([as_blocks(pair_inverse)] + pair_in + [early_cols]), "prow"
    )
    root_all = lax.all_gather(
        jnp.concatenate([as_blocks(root_inverse), as_blocks(root_blocks)]), "prow"
    )

    shared_turned = jnp.transpose(shared_rhs.reshape(-1, tile_rows, rhs_width), (2, 0, 1))
    beyond = jnp.where(lax.axis_index("pcol") == 0, shared_turned.astype(jnp.float32), 0.0)
    within = [None] * panels
    own_solved = []
    for step in range(panels - 1):
        if step == 0:
            partial_value = first_partial
        else:
            residual = own_rows[step].astype(jnp.float32) - row_total(within[step])
            partial_value = inverse_product(own_inv[step], residual)
        result = column_total(partial_value)
        own_solved.append(result)
        for target in range(step + 1, panels):
            block = own_in[step][target - step - 1]
            update = jnp.dot(block, result, preferred_element_type=jnp.float32)
            within[target] = update if within[target] is None else within[target] + update
        beyond = beyond - lax.dot_general(
            result, own_out[step], (((0,), (2,)), ((), ())), preferred_element_type=jnp.float32
        )

    residual = own_rows[-1].astype(jnp.float32) - row_total(within[-1])
    partial_turned = lax.dot_general(
        residual.astype(jnp.bfloat16),
        own_inv[-1],
        (((0,), (0,)), ((), ())),
        preferred_element_type=jnp.float32,
    ).astype(jnp.bfloat16)
    pieces = jnp.concatenate(
        [
            partial_turned.reshape(prows, wide, col_width),
            beyond[:, :panels].astype(jnp.bfloat16).reshape(prows, wide, panels * tile_rows),
        ],
        axis=-1,
    )
    received = lax.all_to_all(pieces, "prow", 0, 0)
    last_own = jnp.sum(received[:, :, :col_width].astype(jnp.float32), axis=0).astype(jnp.bfloat16)
    ancestors = []
    for t in range(panels):
        start = col_width + t * tile_rows
        part = received[:, :, start : start + tile_rows].transpose(1, 0, 2)
        product = transposed_product(last_own, pair_all[:, t - panels])
        ancestors.append(part.astype(jnp.float32) - product)

    pcols = lax.axis_size("pcol")
    halves = ancestors[0].astype(jnp.bfloat16).reshape(2, 1, half, prows, tile_rows)
    pieces = jnp.broadcast_to(halves, (2, pcols, half, prows, tile_rows))
    groups = [
        [layer * pcols + c for layer in (low, low + 1) for c in range(pcols)]
        for low in range(0, layers, 2)
    ]
    partials = lax.all_to_all(
        pieces.reshape((2 * pcols,) + halves.shape[2:]),
        ("layer", "pcol"),
        0,
        0,
        axis_index_groups=groups,
    )
    first = jnp.sum(partials.astype(jnp.float32), axis=0)
    later = jnp.stack(ancestors[1:])
    low, high = later[:, :half], later[:, half:]
    kept = jnp.where(second == 0, low, high)
    given = jnp.where(second == 0, high, low)
    later = kept + layer_swap(given.astype(jnp.bfloat16), 1).astype(jnp.float32)
    pair_solved = slice_solve(first, list(later), pair_all, panels)
    payload = jnp.concatenate([pair_solved.reshape(panels * half, col_width), last_own])
    everywhere = shared_with_all(payload, "prow")
    last_turned = everywhere[:, panels * half :].reshape(rhs_width, col_width)
    mine = everywhere[:, : panels * half]
    theirs = layer_swap(mine, 1)
    pair_turned = jnp.where(
        second == 0, jnp.stack([mine, theirs], axis=1), jnp.stack([theirs, mine], axis=1)
    )
    pair_turned = pair_turned.reshape(prows, 2, panels, half, col_width).transpose(2, 0, 1, 3, 4)

    left = beyond[:, panels:] - transposed_product(last_turned, own_out[-1][panels:])
    mine = mine.reshape(prows, panels, half, col_width).transpose(1, 0, 2, 3)
    mine = mine.reshape(panels, prows * half, col_width)
    taken = sum(transposed_product(mine[step], pair_out[step]) for step in range(panels))
    taken = taken.reshape(prows, 1, half, panels, tile_rows)
    is_mine = jnp.arange(2).reshape(1, 2, 1, 1, 1) == second
    left = left.reshape(prows, 2, half, panels, tile_rows) - jnp.where(is_mine, taken, 0.0)
    pieces = left.astype(jnp.bfloat16).reshape(prows, layers, narrow, panels, tile_rows)
    pieces = pieces.transpose(1, 0, 2, 3, 4)
    by_source = lax.all_to_all(pieces, "layer", 0, 0)
    pieces = jnp.sum(by_source.astype(jnp.float32), axis=0).astype(jnp.bfloat16)
    received = lax.all_to_all(pieces, "prow", 0, 0)
    sums = received.astype(jnp.float32).transpose(1, 0, 2, 3)
    sums = [sums[:, :, t] for t in range(panels)]
    root_solved = slice_solve(row_total(sums[0]), sums[1:], root_all, panels)
    by_layer = shared_with_all(shared_with_all(root_solved, "prow"), "layer")
    root_turned = by_layer.transpose(2, 1, 0, 3, 4).reshape(panels, rhs_width, col_width)

    shape = (1, panels, cycles, 1, tile_rows, rhs_width)
    own_solved.append(last_turned.T)
    return (
        jnp.stack(own_solved).reshape(shape),
        pair_turned.reshape(panels, rhs_width, col_width).transpose(0, 2, 1).reshape(shape),
        root_turned.transpose(0, 2, 1).reshape(shape),
    )


def solution(mesh):
    return jax.shard_map(
        local,
        mesh=mesh,
        in_specs=(
            P("layer", None, "prow", None, None, "pcol", None),
            P("layer", None, "prow", None, "pcol"),
            P("layer", None, "prow", None, None, "pcol", None),
            P("layer", None, "prow", None, None, "pcol", None),
            P("layer", None, "prow", None, None, "pcol", None),
            P(None, "prow", None, None, "pcol", None),
            P(None, "prow", None, None, "pcol", None),
            P("layer", None, "prow", None, None),
            P("layer", None, "prow", None, None),
        ),
        out_specs=(
            P("layer", None, None, "pcol", None, None),
            P("layer", None, None, "pcol", None, None),
            P("layer", None, None, "pcol", None, None),
        ),
        check_vma=False,
    )
```

```python
import jax
import jax.numpy as jnp
from jax import lax
from jax.sharding import PartitionSpec as P


def shared_with_all(value, axis):
    copies = jnp.broadcast_to(value[None], (lax.axis_size(axis),) + value.shape)
    return lax.all_to_all(copies, axis, 0, 0)


def row_total(partial_value):
    partials = shared_with_all(partial_value.astype(jnp.bfloat16), "pcol")
    return jnp.sum(partials.astype(jnp.float32), axis=0)


def transposed_product(solved, blocks):
    return lax.dot_general(
        solved,
        blocks,
        (((solved.ndim - 1,), (blocks.ndim - 1,)), ((), ())),
        preferred_element_type=jnp.float32,
    )


def column_total(partial_value):
    ways = lax.axis_size("prow")
    rows, width = partial_value.shape
    pieces = partial_value.reshape(ways, rows // ways, width)
    received = lax.all_to_all(pieces, "prow", 0, 0)
    piece = jnp.sum(received.astype(jnp.float32), axis=0).astype(jnp.bfloat16)
    return shared_with_all(piece, "prow").reshape(rows, width)


def inverse_product(inverse, residual):
    return lax.dot_general(
        inverse,
        residual.astype(jnp.bfloat16),
        (((0,), (0,)), ((), ())),
        preferred_element_type=jnp.float32,
    ).astype(jnp.bfloat16)


def layer_swap(value, apart):
    return lax.ppermute(value, "layer", [(i, i ^ apart) for i in range(lax.axis_size("layer"))])


def as_blocks(stored):
    tile_rows, cycles = stored.shape[-4], stored.shape[-3]
    return stored.reshape(-1, tile_rows, cycles * stored.shape[-1])


def by_column(cols, panels, chain_length):
    inside, outside = [], []
    offset = 0
    for step in range(panels):
        cut = offset + panels - 1 - step
        inside.append(cols[offset:cut])
        offset += chain_length - 1 - step
        outside.append(cols[cut:offset])
    return inside, outside


def slice_solve(first, sums, gathered, panels):
    sums = [first] + sums
    solved = []
    offset = panels
    for step in range(panels):
        residual = (first if step == 0 else row_total(sums[step])).astype(jnp.bfloat16)
        result = lax.dot_general(
            residual,
            gathered[:, step],
            (((1, 2), (0, 1)), ((), ())),
            preferred_element_type=jnp.float32,
        ).astype(jnp.bfloat16)
        solved.append(result)
        for target in range(step + 1, panels):
            sums[target] = sums[target] - transposed_product(
                result, gathered[:, offset + target - step - 1]
            )
        offset += panels - 1 - step
    return jnp.stack(solved)


def local(
    own_blocks,
    own_pattern,
    own_inverse,
    pair_blocks,
    pair_inverse,
    root_blocks,
    root_inverse,
    own_rhs,
    shared_rhs,
):
    tile_rows = own_blocks.shape[3]
    cycles = own_blocks.shape[4]
    col_width = cycles * tile_rows
    rhs_width = own_rhs.shape[-1]
    panels = own_inverse.shape[1]
    layers, prows = lax.axis_size("layer"), lax.axis_size("prow")
    second = lax.axis_index("layer") % 2
    wide = rhs_width // prows
    half = wide // 2
    narrow = wide // layers

    own_rows = own_rhs.reshape(-1, tile_rows, rhs_width)
    first_inv = own_inverse[0, 0, 0].reshape(tile_rows, col_width)
    first_partial = inverse_product(first_inv, own_rows[0])
    own_inv = own_inverse.reshape(-1, tile_rows, col_width)
    own_tiles = own_blocks.reshape(-1, tile_rows, cycles, tile_rows)
    kept_tiles = own_pattern.reshape(-1, 1, cycles, 1) > 0
    own_cols = jnp.where(kept_tiles, own_tiles, jnp.zeros((), own_tiles.dtype)).reshape(
        -1, tile_rows, col_width
    )
    own_in, own_out = by_column(own_cols, panels, 3 * panels)
    ahead = slice(own_tiles.shape[0] - 2 * panels, own_tiles.shape[0] - panels)
    early_tiles = own_blocks[0, ahead, 0].reshape(-1, tile_rows, cycles, tile_rows)
    early_kept = own_pattern[0, ahead].reshape(-1, 1, cycles, 1) > 0
    early_cols = jnp.where(early_kept, early_tiles, jnp.zeros((), own_tiles.dtype)).reshape(
        -1, tile_rows, col_width
    )
    pair_in, pair_out = by_column(as_blocks(pair_blocks), panels, 2 * panels)
    pair_all = lax.all_gather(
        jnp.concatenate([as_blocks(pair_inverse)] + pair_in + [early_cols]), "prow"
    )
    root_all = lax.all_gather(
        jnp.concatenate([as_blocks(root_inverse), as_blocks(root_blocks)]), "prow"
    )

    shared_turned = jnp.transpose(shared_rhs.reshape(-1, tile_rows, rhs_width), (2, 0, 1))
    beyond = jnp.where(lax.axis_index("pcol") == 0, shared_turned.astype(jnp.float32), 0.0)
    within = [None] * panels
    own_solved = []
    for step in range(panels - 1):
        if step == 0:
            partial_value = first_partial
        else:
            residual = own_rows[step].astype(jnp.float32) - row_total(within[step])
            partial_value = inverse_product(own_inv[step], residual)
        result = column_total(partial_value)
        own_solved.append(result)
        for target in range(step + 1, panels):
            block = own_in[step][target - step - 1]
            update = jnp.dot(block, result, preferred_element_type=jnp.float32)
            within[target] = update if within[target] is None else within[target] + update
        beyond = beyond - lax.dot_general(
            result, own_out[step], (((0,), (2,)), ((), ())), preferred_element_type=jnp.float32
        )

    residual = own_rows[-1].astype(jnp.float32) - row_total(within[-1])
    partial_turned = lax.dot_general(
        residual.astype(jnp.bfloat16),
        own_inv[-1],
        (((0,), (0,)), ((), ())),
        preferred_element_type=jnp.float32,
    ).astype(jnp.bfloat16)
    pieces = jnp.concatenate(
        [
            partial_turned.reshape(prows, wide, col_width),
            beyond[:, :panels].astype(jnp.bfloat16).reshape(prows, wide, panels * tile_rows),
        ],
        axis=-1,
    )
    received = lax.all_to_all(pieces, "prow", 0, 0)
    last_own = jnp.sum(received[:, :, :col_width].astype(jnp.float32), axis=0).astype(jnp.bfloat16)
    ancestors = []
    for t in range(panels):
        start = col_width + t * tile_rows
        part = received[:, :, start : start + tile_rows].transpose(1, 0, 2)
        product = transposed_product(last_own, pair_all[:, t - panels])
        ancestors.append(part.astype(jnp.float32) - product)

    pcols = lax.axis_size("pcol")
    halves = ancestors[0].astype(jnp.bfloat16).reshape(2, 1, half, prows, tile_rows)
    pieces = jnp.broadcast_to(halves, (2, pcols, half, prows, tile_rows))
    groups = [
        [layer * pcols + c for layer in (low, low + 1) for c in range(pcols)]
        for low in range(0, layers, 2)
    ]
    partials = lax.all_to_all(
        pieces.reshape((2 * pcols,) + halves.shape[2:]),
        ("layer", "pcol"),
        0,
        0,
        axis_index_groups=groups,
    )
    first = jnp.sum(partials.astype(jnp.float32), axis=0)
    later = jnp.stack(ancestors[1:])
    low, high = later[:, :half], later[:, half:]
    kept = jnp.where(second == 0, low, high)
    given = jnp.where(second == 0, high, low)
    later = kept + layer_swap(given.astype(jnp.bfloat16), 1).astype(jnp.float32)
    pair_solved = slice_solve(first, list(later), pair_all, panels)
    payload = jnp.concatenate([pair_solved.reshape(panels * half, col_width), last_own])
    everywhere = shared_with_all(payload, "prow")
    last_turned = everywhere[:, panels * half :].reshape(rhs_width, col_width)
    mine = everywhere[:, : panels * half]
    theirs = layer_swap(mine, 1)
    pair_turned = jnp.where(
        second == 0, jnp.stack([mine, theirs], axis=1), jnp.stack([theirs, mine], axis=1)
    )
    pair_turned = pair_turned.reshape(prows, 2, panels, half, col_width).transpose(2, 0, 1, 3, 4)

    left = beyond[:, panels:] - transposed_product(last_turned, own_out[-1][panels:])
    mine = mine.reshape(prows, panels, half, col_width).transpose(1, 0, 2, 3)
    mine = mine.reshape(panels, prows * half, col_width)
    taken = sum(transposed_product(mine[step], pair_out[step]) for step in range(panels))
    taken = taken.reshape(prows, 1, half, panels, tile_rows)
    is_mine = jnp.arange(2).reshape(1, 2, 1, 1, 1) == second
    left = left.reshape(prows, 2, half, panels, tile_rows) - jnp.where(is_mine, taken, 0.0)
    pieces = left.astype(jnp.bfloat16).reshape(prows, layers, narrow, panels, tile_rows)
    pieces = pieces.transpose(1, 0, 2, 3, 4)
    by_source = lax.all_to_all(pieces, "layer", 0, 0)
    pieces = jnp.sum(by_source.astype(jnp.float32), axis=0).astype(jnp.bfloat16)
    received = lax.all_to_all(pieces, "prow", 0, 0)
    sums = received.astype(jnp.float32).transpose(1, 0, 2, 3)
    sums = [sums[:, :, t] for t in range(panels)]
    root_solved = slice_solve(row_total(sums[0]), sums[1:], root_all, panels)
    by_layer = shared_with_all(shared_with_all(root_solved, "prow"), "layer")
    root_turned = by_layer.transpose(2, 1, 0, 3, 4).reshape(panels, rhs_width, col_width)

    shape = (1, panels, cycles, 1, tile_rows, rhs_width)
    own_solved.append(last_turned.T)
    return (
        jnp.stack(own_solved).reshape(shape),
        pair_turned.reshape(panels, rhs_width, col_width).transpose(0, 2, 1).reshape(shape),
        root_turned.transpose(0, 2, 1).reshape(shape),
    )


def solution(mesh):
    return jax.shard_map(
        local,
        mesh=mesh,
        in_specs=(
            P("layer", None, "prow", None, None, "pcol", None),
            P("layer", None, "prow", None, "pcol"),
            P("layer", None, "prow", None, None, "pcol", None),
            P("layer", None, "prow", None, None, "pcol", None),
            P("layer", None, "prow", None, None, "pcol", None),
            P(None, "prow", None, None, "pcol", None),
            P(None, "prow", None, None, "pcol", None),
            P("layer", None, "prow", None, None),
            P("layer", None, "prow", None, None),
        ),
        out_specs=(
            P("layer", None, None, "pcol", None, None),
            P("layer", None, None, "pcol", None, None),
            P("layer", None, None, "pcol", None, None),
        ),
        check_vma=False,
    )
```
